32 devices in a mesh: gx: 4 (over y, x), gy: 4 (over z), gz: 2 (over core).
Axes of the slice: x: 2, y: 2, z: 4, core: 2. Of those that a mesh axis runs over, the one named last changes fastest.
Arguments:
- well_sources: float32 [1536, 64], P(('gx', 'gy'), 'gz'), may hold values from -6 to 6
- well_owner: int32 [1536, 1], P(('gx', 'gy')), may hold values from 0 to 15; in each aligned block of 96 rows (0 to 95, 96 to 191, ...) at most 12 rows name the same one
- well_cell: int32 [1536], P(('gx', 'gy')), may hold values from 0 to 2047
- flow_sign: int32 [3, 64, 64, 512], P(None, 'gz', 'gx', 'gy'), may hold values from 0 to 7
- courant: float32 [3, 64, 64, 512], P(None, 'gz', 'gx', 'gy'), may hold values from 0.01 to 0.3
- tracer: float32 [3, 64, 64, 512], P(None, 'gz', 'gx', 'gy'), may hold values from -6 to 6
Outputs:
- lambda_start: float32 [64, 64, 512], P('gz', 'gx', 'gy')
- smoothed: float32 [512, 64, 64], P(('gx', 'gy', 'gz'))
The draws below stay inside these ranges and needn't reach their ends.
Inputs may be any that keep to these rules, and one draw needn't show every extreme that they name: `well_owner`: among the wells of one index of gx+gy at most 12 name the same owner, a bound that some block of them reaches.
All inputs are finite; a program needn't handle non-finite values.
Results may differ from the reference program's by a relative error of at most 0.00015.
Values sent between devices are 32-bit elements; how exact they have to be, the bound alone decides.
A program may use at most 128 MiB of HBM per device.

```python
import math
import jax
import jax.numpy as jnp
import numpy as np
from jax import lax

CX = 16
CY = 128
STEPS = 3
WELL_DEV = 96
CAP = 12
NX = 64
NY = 512
NZ = 64
WELLS = 1536
LX = 32
LY = 256
LZ = 64
N_GX = 4
N_GY = 4


def set_ends(drawn, own_key, least, largest):
    shape = drawn.shape
    index_at = [jax.random.randint(jax.random.fold_in(own_key, axis), (), 0, shape[axis]) for axis in range(len(shape))]
    drawn = drawn.at[tuple(index_at)].set(least)
    longest = shape.index(max(shape))
    index_at[longest] = (index_at[longest] + 1) % shape[longest]
    return drawn.at[tuple(index_at)].set(largest)


def levels(rng, dims, pieces, least, high):
    factor_of, own = 1.0, jax.random.fold_in(rng, 6)
    for dim, blocks in pieces:
        heights = jnp.exp(jax.random.uniform(jax.random.fold_in(own, dim), (blocks,), jnp.float32, least / len(pieces), high / len(pieces)))
        factor_of = factor_of * jnp.repeat(heights, dims[dim] // blocks).reshape([-1 if axis == dim else 1 for axis in range(len(dims))])
    return factor_of


def deal_out(key, own, number, rows, amount, top, limit, lean):
    sequence = jax.random.permutation(key, amount)
    crowded, common = load_shares(amount, rows * top, limit, lean, True), load_shares(amount, rows * top, limit, lean, False)
    places = jnp.arange(amount)

    def named(lengths, offset_by):
        used = int((lengths > 0).sum())
        fixed = max(1, used // 4)
        moved = fixed + (places - fixed + offset_by * (used - fixed)) % max(1, amount - fixed)
        return jnp.zeros((amount,), jnp.int32).at[sequence[jnp.where(places < fixed, places, moved)]].set(jnp.asarray(lengths, jnp.int32))

    lengths = jnp.where(number % 4 == 0, named(crowded, number // 4), named(common, number - number // 4 - 1))
    mixed = jax.random.permutation(jax.random.fold_in(own, 3), amount)
    giver, receiver = mixed[0:amount // 2 * 2:2], mixed[1:amount // 2 * 2:2]
    margin = jnp.minimum(lengths[giver] - 1, limit - lengths[receiver]) // 2
    margin = jnp.where((giver == sequence[0]) | (receiver == sequence[0]) | (lengths[receiver] == 0), 0, jnp.maximum(margin, 0))
    moved = jax.random.randint(jax.random.fold_in(own, 4), (amount // 2,), 0, 1 << 20) % (margin + 1)
    lengths = lengths.at[giver].add(-moved).at[receiver].add(moved)
    items = jnp.searchsorted(jnp.cumsum(lengths), jnp.arange(rows * top), side="right").astype(jnp.int32)
    grid = items.reshape(top, rows).T
    grid = grid[jax.random.permutation(jax.random.fold_in(own, 1), rows)]
    offset_by = jax.random.randint(jax.random.fold_in(own, 2), (rows, 1), 0, top)
    return jnp.take_along_axis(grid, (jnp.arange(top)[None, :] + offset_by) % top, axis=1)


def load_shares(amount, total, most, lean, full):
    weights = [(1 << 20) // math.isqrt(rank ** lean) + 1 for rank in range(1, amount + 1)]
    largest = most if full else min(most, max(-(-total // amount), total * weights[0] // sum(weights)))
    least = 1 if total - largest >= amount - 1 else 0
    counts, surplus = [largest] + [least] * (amount - 1), total - largest - least * (amount - 1)
    while surplus > 0:
        movable = [i for i in range(1, amount) if counts[i] < largest] or [i for i in range(1, amount) if counts[i] < most]
        pool, left = sum([weights[i] for i in movable]), surplus
        for i in movable:
            extra = min(most - counts[i], max(1, left * weights[i] // pool), surplus)
            counts[i] = counts[i] + extra
            surplus = surplus - extra
    return np.array(counts)


def normal_values(stream_key, shape, width, bound, cuts=(), kind=jnp.bfloat16):
    level = levels(stream_key, shape, cuts, -0.22, 0.18) if cuts else 1.0
    result = jax.random.normal(stream_key, shape, jnp.float32) * width * level
    return jnp.minimum(jnp.maximum(result, -bound), bound).astype(kind)


def setup_inputs(seed: int = 0) -> dict:
    arg_keys = jax.random.split(jax.random.key(seed), 7)
    well_sources = normal_values(arg_keys[0], (WELLS, NZ), 1.0, 6.0, ((0, 16), (1, 2)), jnp.float32)
    well_owner_keys = jax.random.split(jax.random.fold_in(arg_keys[1], 1), WELLS // WELL_DEV)
    well_owner_turns = jax.random.permutation(jax.random.fold_in(arg_keys[1], 3), WELLS // WELL_DEV)
    well_owner = jax.vmap(lambda own, number: deal_out(jax.random.fold_in(arg_keys[1], 2), own, number, WELL_DEV, N_GX * N_GY, 1, CAP, 2))(well_owner_keys, well_owner_turns).reshape((WELLS, 1))
    well_cell = set_ends(jax.random.randint(arg_keys[2], (WELLS,), 0, CX * CY), jax.random.fold_in(arg_keys[2], 1), 0, (CX * CY) - 1).astype(jnp.int32)
    flow_sign = set_ends(jax.random.randint(arg_keys[3], (STEPS, NZ, NX, NY), 0, 8), jax.random.fold_in(arg_keys[3], 1), 0, 7).astype(jnp.int32)
    courant = jnp.clip(jnp.exp(math.log(0.3) - 3.4011974 * jax.random.uniform(arg_keys[4], (3, NZ, NX, NY), jnp.float32) ** levels(arg_keys[4], (3, NZ, NX, NY), ((1, 2), (2, 4), (3, 4)), -0.2, 0.2)), 0.01, 0.3)
    tracer = normal_values(arg_keys[5], (STEPS, NZ, NX, NY), 1.0, 6.0, ((1, 2), (2, 4), (3, 4)), jnp.float32)
    return {"well_sources": well_sources, "well_owner": well_owner, "well_cell": well_cell, "flow_sign": flow_sign, "courant": courant, "tracer": tracer}


def correlation(extent, length):
    places = jnp.arange(extent).astype(jnp.float32)
    spacing = jnp.abs(places[:, None] - places[None, :])
    return jnp.exp(-spacing / length) / math.sqrt(length)

def from_above(values, along_dim):
    extent = values.shape[along_dim]
    inside = lax.slice_in_dim(values, 1, extent, axis=along_dim)
    border = jnp.zeros_like(lax.slice_in_dim(values, 0, 1, axis=along_dim))
    return jnp.concatenate([inside, border], axis=along_dim)

def from_below(values, along_dim):
    extent = values.shape[along_dim]
    inside = lax.slice_in_dim(values, 0, extent - 1, axis=along_dim)
    border = jnp.zeros_like(lax.slice_in_dim(values, 0, 1, axis=along_dim))
    return jnp.concatenate([border, inside], axis=along_dim)

def reference(well_sources, well_owner, well_cell, flow_sign, courant, tracer):
    owners = well_owner[:, 0]
    well_x = owners // N_GY * CX + well_cell // CY
    well_y = owners % N_GY * CY + well_cell % CY
    adjoint = jnp.zeros((NZ, NX, NY), jnp.float32).at[:, well_x, well_y].add(jnp.transpose(well_sources))
    staying = 1.0 - (courant[0] + courant[1] + courant[2])
    gradient = jnp.zeros((NZ, NX, NY), jnp.float32)
    for step in reversed(range(STEPS)):
        packed = flow_sign[step]
        updated = staying * adjoint
        for component, along_dim in ((0, 1), (1, 2), (2, 0)):
            upward = (packed // 2 ** component % 2).astype(jnp.float32)
            rising = courant[component] * upward
            falling = courant[component] * (1.0 - upward)
            updated = updated + from_above(rising * adjoint, along_dim) + from_below(falling * adjoint, along_dim)
        adjoint = updated
        gradient = gradient + adjoint * tracer[step]
    highest = lax.Precision.HIGHEST
    smooth_y = jnp.einsum('zxj,ij->zxi', gradient, correlation(NY, LY), precision=highest)
    smooth_x = jnp.einsum('zjy,ij->ziy', smooth_y, correlation(NX, LX), precision=highest)
    smoothed = jnp.einsum('jxy,ij->yix', smooth_x, correlation(NZ, LZ), precision=highest)
    return (adjoint, smoothed)
```

```python
import functools
import math

import jax
import jax.numpy as jnp
from jax import lax
from jax.experimental import pallas as pl
from jax.experimental.pallas import tpu as pltpu
from jax.sharding import PartitionSpec as P

MESH = pl.DeviceIdType.MESH
LANES = 128
ROWS = 8


def round_up(value, unit):
    return -(-value // unit) * unit


def iota(shape, dim):
    return lax.broadcasted_iota(jnp.int32, shape, dim)


def parts(value):
    high = value.astype(jnp.bfloat16)
    return high, (value - high.astype(jnp.float32)).astype(jnp.bfloat16)


def dot(left, right, dims):
    return lax.dot_general(left, right, (dims, ((), ())), preferred_element_type=jnp.float32)


NN = ((1,), (0,))
NT = ((1,), (1,))
TN = ((0,), (0,))


def flag(mask):
    return jnp.where(mask, 1.0, 0.0).astype(jnp.bfloat16)


def dot_three(left, right, dims):
    left_high, left_low = parts(left)
    right_high, right_low = parts(right)
    return (
        dot(left_high, right_high, dims)
        + dot(left_low, right_high, dims)
        + dot(left_high, right_low, dims)
    )


def kernel(
    sizes, source_ref, owner_ref, cell_ref, flow_any, courant_any, tracer_any,
    lambda_ref, smooth_ref,
    flow_ref, courant_ref, tracer_ref, load_sem,
    payload_ref, well_send, well_recv, well_send_sem, well_recv_sem,
    rise_ref, fall_ref, sum_ref, grad_ref,
    x_send, x_recv, y_send, y_recv, z_send, z_recv, face_send_sem, face_recv_sem,
    carry_send, carry_recv, carry_send_sem, carry_recv_sem,
    bulk_send, bulk_recv, bulk_send_sem, bulk_recv_sem,
    table_high, table_low, wide_ref, stage_ref=None,
):
    n_gx, n_gy, n_gz, brick_z, brick_x, brick_y, cap = sizes
    steps = flow_any.shape[0]
    lines = brick_z * brick_x
    groups = n_gx * n_gy
    devices = groups * n_gz
    a, b, c = lax.axis_index("gx"), lax.axis_index("gy"), lax.axis_index("gz")
    group = a * n_gy + b
    me = group * n_gz + c
    wells = source_ref.shape[1]
    full_z = n_gz * brick_z
    full_x = n_gx * brick_x
    wide_x = round_up(full_x, LANES)
    shares = n_gx * n_gz
    y_rows = brick_y // shares
    pad_rows = round_up(y_rows, ROWS)
    tiles = lines // LANES
    tile_z = LANES // brick_x

    loads = [
        pltpu.make_async_copy(src, dst, load_sem.at[i])
        for i, (src, dst) in enumerate(
            ((courant_any, courant_ref), (flow_any, flow_ref), (tracer_any, tracer_ref))
        )
    ]
    for load in loads:
        load.start()

    for ref in (x_recv, y_recv, z_recv, carry_recv):
        ref[...] = jnp.zeros_like(ref)

    barrier = pltpu.get_barrier_semaphore()

    def greet(d, carried):
        other = lax.rem(me + d, devices)
        pl.semaphore_signal(
            barrier, inc=1,
            device_id=(
                lax.div(other, n_gy * n_gz), lax.rem(lax.div(other, n_gz), n_gy), lax.rem(other, n_gz)
            ),
            device_id_type=MESH,
        )
        return carried

    lax.fori_loop(1, devices, greet, 0)

    eye = iota((wells, wells), 0) == iota((wells, wells), 1)
    before = iota((wells, wells), 0) < iota((wells, wells), 1)
    owner_row = owner_ref[...].astype(jnp.float32)
    owner_col = jnp.sum(jnp.where(eye, owner_row, 0.0), axis=1, keepdims=True)
    rank_row = jnp.sum(
        jnp.where(before & (owner_col == owner_row), 1.0, 0.0), axis=0, keepdims=True
    )
    key_row = (owner_row * cap + rank_row).astype(jnp.int32)
    chosen = flag(iota((groups * cap, wells), 0) == key_row)
    cell_row = cell_ref[...]
    payload_ref[...] = jnp.zeros_like(payload_ref)
    payload_ref[0:brick_z, :] = source_ref[...]
    payload_ref[brick_z:brick_z + 1, :] = lax.div(cell_row, brick_y).astype(jnp.float32)
    payload_ref[brick_z + 1:brick_z + 2, :] = lax.rem(cell_row, brick_y).astype(jnp.float32)
    payload_high, payload_low = parts(payload_ref[...])
    well_send[...] = dot(chosen, payload_high, NT) + dot(chosen, payload_low, NT)

    pl.semaphore_wait(barrier, devices - 1)

    def group_rows(index):
        return pl.ds(pl.multiple_of(index * cap, ROWS), cap)

    def well_copy(d):
        other = lax.rem(group + d, groups)
        return pltpu.make_async_remote_copy(
            src_ref=well_send.at[group_rows(other), :],
            dst_ref=well_recv.at[group_rows(group), :],
            send_sem=well_send_sem.at[d],
            recv_sem=well_recv_sem.at[d],
            device_id=(lax.div(other, n_gy), lax.rem(other, n_gy), c),
            device_id_type=MESH,
        )

    def well_start(d, carried):
        well_copy(d).start()
        return carried

    lax.fori_loop(1, groups, well_start, 0)
    well_recv[group_rows(group), :] = well_send[group_rows(group), :]

    shape = (n_gx * LANES, wide_x)
    at_x = lax.div(iota(shape, 0), LANES) * brick_x + lax.rem(iota(shape, 0), brick_x)
    far = jnp.abs(at_x - iota(shape, 1)).astype(jnp.float32)
    table = jnp.exp(far * (-0.5 / brick_x)) / math.sqrt(2 * brick_x) / math.sqrt(2 * brick_z)
    table = jnp.where(iota(shape, 1) < full_x, table, 0.0)
    depth_of = lax.rem(lax.div(iota(shape, 0), brick_x), tile_z)
    for depth in range(tile_z):
        high, low = parts(jnp.where(depth_of == depth, table, 0.0))
        table_high[:, depth * wide_x:(depth + 1) * wide_x] = high
        table_low[:, depth * wide_x:(depth + 1) * wide_x] = low

    slots = groups * cap
    spread = flag(lax.div(iota((lines, LANES), 0), brick_x) == iota((lines, LANES), 1))
    x_pick = flag(iota((ROWS, LANES), 1) == brick_z)

    loads[0].wait()
    loads[1].wait()
    loads[2].wait()

    def well_wait(d, carried):
        copy = well_copy(d)
        copy.wait_send()
        copy.wait_recv()
        return carried

    lax.fori_loop(1, groups, well_wait, 0)
    landed = well_recv[...]
    landed_high, landed_low = parts(landed)
    x_row = dot(x_pick, landed_high, NT)[0:1, :].astype(jnp.int32)
    x_hit = lax.rem(iota((lines, slots), 0), brick_x) == x_row
    y_hit = flag(
        iota((slots, LANES), 1) == landed[:, brick_z + 1:brick_z + 2].astype(jnp.int32)
    )
    spread_high = jnp.where(x_hit, dot(spread, landed_high, NT), 0.0).astype(jnp.bfloat16)
    spread_low = jnp.where(x_hit, dot(spread, landed_low, NT), 0.0).astype(jnp.bfloat16)
    adjoint = dot(spread_high, y_hit, NN) + dot(spread_low, y_hit, NN)

    y_pos = iota((lines, brick_y), 1)
    x_pos = lax.rem(iota((lines, brick_y), 0), brick_x)
    take_row, take_lane = iota((2 * ROWS, brick_y), 0), iota((2 * ROWS, brick_y), 1)
    take = flag(
        ((take_row < ROWS) & (take_lane == 0)) | ((take_row >= ROWS) & (take_lane == brick_y - 1))
    )
    put = flag(
        ((take_row == 0) & (take_lane == brick_y - 1)) | ((take_row == ROWS) & (take_lane == 0))
    )

    def face_copies(step):
        copies = []
        for axis, (place, count, send, recv) in enumerate(
            ((a, n_gx, x_send, x_recv), (b, n_gy, y_send, y_recv), (c, n_gz, z_send, z_recv))
        ):
            for side in range(2):
                moved = place - 1 if side == 0 else place + 1
                target = [a, b, c]
                target[axis] = lax.rem(moved + count, count)
                sends = place > 0 if side == 0 else place < count - 1
                gets = place < count - 1 if side == 0 else place > 0
                copy = pltpu.make_async_remote_copy(
                    src_ref=send.at[step, side],
                    dst_ref=recv.at[step, side],
                    send_sem=face_send_sem.at[step, axis, side],
                    recv_sem=face_recv_sem.at[step, axis, side],
                    device_id=tuple(target),
                    device_id_type=MESH,
                )
                copies.append((copy, sends, gets))
        return copies

    def when_start(copy, sends):
        @pl.when(sends)
        def _():
            copy.start()

    all_copies = []
    for step in reversed(range(steps)):
        copies = face_copies(step)
        all_copies.extend(copies)
        flow = flow_ref[step]
        flows = [courant_ref[axis] * adjoint for axis in range(3)]
        rise = [
            jnp.where((flow & (1 << axis)) != 0, flows[axis], 0.0) for axis in range(3)
        ]
        fall = [flows[axis] - rise[axis] for axis in range(3)]
        edge = jnp.where(y_pos == 0, rise[1], jnp.where(y_pos == brick_y - 1, fall[1], 0.0))
        edge_high, edge_low = parts(edge)
        edge_rows = dot(take, edge_high, NT) + dot(take, edge_low, NT)
        y_send[step, 0] = edge_rows[0:ROWS]
        y_send[step, 1] = edge_rows[ROWS:2 * ROWS]
        when_start(*copies[2][:2])
        when_start(*copies[3][:2])
        rise_ref[...] = rise[0]
        fall_ref[...] = fall[0]
        x_send[step, 0] = rise_ref[pl.ds(0, brick_z, stride=brick_x), :]
        x_send[step, 1] = fall_ref[pl.ds(brick_x - 1, brick_z, stride=brick_x), :]
        when_start(*copies[0][:2])
        when_start(*copies[1][:2])
        z_send[step, 0] = rise[2][0:brick_x]
        z_send[step, 1] = fall[2][lines - brick_x:lines]
        when_start(*copies[4][:2])
        when_start(*copies[5][:2])

        rest = 1.0 - (courant_ref[0] + courant_ref[1] + courant_ref[2])
        updated = rest * adjoint
        updated = updated + jnp.where(
            x_pos == brick_x - 1, 0.0, pltpu.roll(rise[0], lines - 1, 0)
        )
        updated = updated + jnp.where(x_pos == 0, 0.0, pltpu.roll(fall[0], 1, 0))
        updated = updated + jnp.where(
            y_pos == brick_y - 1, 0.0, pltpu.roll(rise[1], brick_y - 1, 1)
        )
        updated = updated + jnp.where(y_pos == 0, 0.0, pltpu.roll(fall[1], 1, 1))
        border = jnp.zeros((brick_x, brick_y), jnp.float32)
        updated = updated + jnp.concatenate([rise[2][brick_x:], border], axis=0)
        updated = updated + jnp.concatenate([border, fall[2][:lines - brick_x]], axis=0)
        sum_ref[...] = updated

        for copy, _, gets in copies:
            @pl.when(gets)
            def _():
                copy.wait_recv()

        top = pl.ds(brick_x - 1, brick_z, stride=brick_x)
        bottom = pl.ds(0, brick_z, stride=brick_x)
        sum_ref[top, :] = sum_ref[top, :] + x_recv[step, 0]
        sum_ref[bottom, :] = sum_ref[bottom, :] + x_recv[step, 1]
        last = pl.ds(lines - brick_x, brick_x)
        sum_ref[last, :] = sum_ref[last, :] + z_recv[step, 0]
        first = pl.ds(0, brick_x)
        sum_ref[first, :] = sum_ref[first, :] + z_recv[step, 1]
        side_rows = jnp.concatenate([y_recv[step, 0], y_recv[step, 1]], axis=0)
        side_high, side_low = parts(side_rows)
        adjoint = sum_ref[...] + (dot(side_high, put, TN) + dot(side_low, put, TN))
        if step == steps - 1:
            gradient = adjoint * tracer_ref[step]
        else:
            gradient = grad_ref[...] + adjoint * tracer_ref[step]
        grad_ref[...] = gradient

    length = 2.0 * brick_y
    from_end = jnp.where(take_row < ROWS, brick_y - take_lane, take_lane + 1)
    pull = jnp.exp(from_end.astype(jnp.float32) * (-1.0 / length)) / math.sqrt(length)
    carries = dot_three(pull, gradient, NT)
    carry_send[0] = carries[0:ROWS]
    carry_send[1] = carries[ROWS:2 * ROWS]
    carry_copies = []
    for d in range(1, n_gy):
        for side in range(2):
            moved = b + d if side == 0 else b - d
            back = b - d if side == 0 else b + d
            copy = pltpu.make_async_remote_copy(
                src_ref=carry_send.at[side],
                dst_ref=carry_recv.at[pl.ds(pl.multiple_of(b * ROWS, ROWS), ROWS), :],
                send_sem=carry_send_sem.at[side, d],
                recv_sem=carry_recv_sem.at[side, d],
                device_id=(a, lax.rem(moved + n_gy, n_gy), c),
                device_id_type=MESH,
            )
            sends = (moved >= 0) & (moved < n_gy)
            gets = (back >= 0) & (back < n_gy)
            when_start(copy, sends)
            carry_copies.append((copy, sends, gets))

    lambda_ref[...] = adjoint

    def line_place(row):
        return lax.div(row, pad_rows) * y_rows + lax.rem(row, pad_rows)

    shape = (shares * pad_rows, brick_y)
    near = jnp.abs(line_place(iota(shape, 0)) - iota(shape, 1)).astype(jnp.float32)
    table_y = jnp.exp(near * (-1.0 / length)) / math.sqrt(length)
    local = dot_three(table_y, gradient, NT)

    shape = (shares * pad_rows, n_gy * ROWS)
    at_y = line_place(iota(shape, 0))
    brick = lax.div(iota(shape, 1), ROWS)
    gap = jnp.where(
        brick < b,
        at_y + brick_y * (b - brick - 1),
        brick_y - 1 - at_y + brick_y * (brick - b - 1),
    )
    useful = (lax.rem(iota(shape, 1), ROWS) == 0) & (brick != b)
    gap = jnp.where(useful, gap, 0)
    push = jnp.where(useful, jnp.exp(gap.astype(jnp.float32) * (-1.0 / length)), 0.0)

    for copy, _, gets in carry_copies:
        @pl.when(gets)
        def _():
            copy.wait_recv()

    bulk_send[...] = local + dot_three(push, carry_recv[...], NN)

    mine = a * n_gz + c

    def bulk_copy(d):
        share = lax.rem(mine + d, shares)
        other = b * shares + share
        return other, pltpu.make_async_remote_copy(
            src_ref=bulk_send.at[pl.ds(pl.multiple_of(share * pad_rows, ROWS), pad_rows), :],
            dst_ref=bulk_recv.at[mine],
            send_sem=bulk_send_sem.at[share],
            recv_sem=bulk_recv_sem.at[mine],
            device_id=(
                lax.div(other, n_gy * n_gz), lax.rem(lax.div(other, n_gz), n_gy), lax.rem(other, n_gz)
            ),
            device_id_type=MESH,
        )

    def bulk_start(d, carried):
        other, copy = bulk_copy(d)

        @pl.when(other != me)
        def _():
            copy.start()

        return carried

    lax.fori_loop(0, shares, bulk_start, 0)

    own = lax.div(me, shares) == b

    @pl.when(own)
    def _():
        rows = pl.ds(pl.multiple_of((me - b * shares) * pad_rows, ROWS), pad_rows)
        bulk_recv[mine] = bulk_send[rows, :]

    for copy, sends, _ in all_copies + carry_copies:
        @pl.when(sends)
        def _():
            copy.wait_send()

    def bulk_wait(d, carried):
        share = lax.rem(mine + d, shares)

        @pl.when(jnp.logical_not(own & (share == mine)))
        def _():
            pltpu.make_async_remote_copy(
                src_ref=bulk_send.at[pl.ds(0, pad_rows), :],
                dst_ref=bulk_recv.at[share],
                send_sem=bulk_send_sem.at[share],
                recv_sem=bulk_recv_sem.at[share],
                device_id=(a, b, c),
                device_id_type=MESH,
            ).wait_recv()

        return carried

    lax.fori_loop(0, shares, bulk_wait, 0)

    rows = [
        jnp.concatenate(
            [
                bulk_recv[i * n_gz + k, :, t * LANES:(t + 1) * LANES]
                for i in range(n_gx)
            ],
            axis=1,
        )
        for k in range(n_gz)
        for t in range(tiles)
    ]
    high, low = parts(jnp.concatenate(rows, axis=0))
    wide_ref[...] = (
        dot(high, table_high[...], NN)
        + dot(low, table_high[...], NN)
        + dot(high, table_low[...], NN)
    )

    fade = math.exp(-0.5 / brick_z)

    def plane(z):
        row, depth = z // tile_z * pad_rows, z % tile_z
        return wide_ref[row:row + y_rows, depth * wide_x:(depth + 1) * wide_x]

    ahead = [plane(0)]
    for z in range(1, full_z):
        ahead.append(plane(z) + fade * ahead[-1])
    behind = None
    for z in reversed(range(full_z)):
        total = ahead[z] if behind is None else ahead[z] + behind
        if full_x <= LANES:
            smooth_ref[pl.ds(z, y_rows, stride=full_z), :] = total[:, 0:full_x]
        else:
            for tile in range(wide_x // LANES):
                part = total[:, tile * LANES:(tile + 1) * LANES]
                stage_ref[tile, pl.ds(z, y_rows, stride=full_z), :] = part
        behind = fade * (plane(z) if behind is None else plane(z) + behind)

    if full_x > LANES:
        for tile in range(wide_x // LANES):
            end = min((tile + 1) * LANES, full_x)
            smooth_ref[:, tile * LANES:end] = stage_ref[tile][:, 0:end - tile * LANES]

    def bulk_sent(d, carried):
        other, copy = bulk_copy(d)

        @pl.when(other != me)
        def _():
            copy.wait_send()

        return carried

    lax.fori_loop(0, shares, bulk_sent, 0)


def per_device(well_sources, well_owner, well_cell, flow_sign, courant, tracer):
    steps, brick_z, brick_x, brick_y = tracer.shape
    n_gx, n_gy, n_gz = lax.axis_size("gx"), lax.axis_size("gy"), lax.axis_size("gz")
    groups, shares = n_gx * n_gy, n_gx * n_gz
    wells = well_cell.shape[0]
    cap = round_up(2 * -(-wells // groups), ROWS)
    lines = brick_z * brick_x
    y_rows = brick_y // shares
    pad_rows = round_up(y_rows, ROWS)
    full_x, full_z = n_gx * brick_x, n_gz * brick_z
    wide_x = round_up(full_x, LANES)
    tile_z = LANES // brick_x
    tiles = lines // LANES
    f32 = jnp.float32
    sizes = (n_gx, n_gy, n_gz, brick_z, brick_x, brick_y, cap)
    dma = pltpu.SemaphoreType.DMA
    vmem = pl.BlockSpec(memory_space=pltpu.VMEM)
    away = pl.BlockSpec(memory_space=pl.ANY)
    field = (3, lines, brick_y)
    stage = []
    if full_x > LANES:
        stage = [pltpu.VMEM((wide_x // LANES, y_rows * full_z, LANES), f32)]
    run = pl.pallas_call(
        functools.partial(kernel, sizes),
        out_shape=(
            jax.ShapeDtypeStruct((lines, brick_y), f32),
            jax.ShapeDtypeStruct((y_rows * full_z, full_x), f32),
        ),
        in_specs=[vmem, vmem, vmem, away, away, away],
        out_specs=(vmem, vmem),
        scratch_shapes=[
            pltpu.VMEM((steps, lines, brick_y), jnp.int32),
            pltpu.VMEM(field, f32),
            pltpu.VMEM((steps, lines, brick_y), f32),
            dma((3,)),
            pltpu.VMEM((LANES, wells), f32),
            pltpu.VMEM((groups * cap, LANES), f32),
            pltpu.VMEM((groups * cap, LANES), f32),
            dma((groups,)),
            dma((groups,)),
            pltpu.VMEM((lines, brick_y), f32),
            pltpu.VMEM((lines, brick_y), f32),
            pltpu.VMEM((lines, brick_y), f32),
            pltpu.VMEM((lines, brick_y), f32),
            pltpu.VMEM((steps, 2, brick_z, brick_y), f32),
            pltpu.VMEM((steps, 2, brick_z, brick_y), f32),
            pltpu.VMEM((steps, 2, ROWS, lines), f32),
            pltpu.VMEM((steps, 2, ROWS, lines), f32),
            pltpu.VMEM((steps, 2, brick_x, brick_y), f32),
            pltpu.VMEM((steps, 2, brick_x, brick_y), f32),
            dma((steps, 3, 2)),
            dma((steps, 3, 2)),
            pltpu.VMEM((2, ROWS, lines), f32),
            pltpu.VMEM((n_gy * ROWS, lines), f32),
            dma((2, n_gy)),
            dma((2, n_gy)),
            pltpu.VMEM((shares * pad_rows, lines), f32),
            pltpu.VMEM((shares, pad_rows, lines), f32),
            dma((shares,)),
            dma((shares,)),
            pltpu.VMEM((n_gx * LANES, tile_z * wide_x), jnp.bfloat16),
            pltpu.VMEM((n_gx * LANES, tile_z * wide_x), jnp.bfloat16),
            pltpu.VMEM((n_gz * tiles * pad_rows, tile_z * wide_x), f32),
        ] + stage,
        compiler_params=pltpu.CompilerParams(
            collective_id=0, has_side_effects=True, vmem_limit_bytes=56 * 2**20
        ),
    )
    start, smoothed = run(
        well_sources.T,
        well_owner.reshape(1, wells),
        well_cell.reshape(1, wells),
        flow_sign.reshape(steps, lines, brick_y),
        courant.reshape(field),
        tracer.reshape(steps, lines, brick_y),
    )
    return (
        start.reshape(brick_z, brick_x, brick_y),
        smoothed.reshape(y_rows, full_z, full_x),
    )


def solution(mesh):
    return jax.shard_map(
        per_device,
        mesh=mesh,
        in_specs=(
            P(("gx", "gy"), "gz"),
            P(("gx", "gy"), None),
            P(("gx", "gy")),
            P(None, "gz", "gx", "gy"),
            P(None, "gz", "gx", "gy"),
            P(None, "gz", "gx", "gy"),
        ),
        out_specs=(P("gz", "gx", "gy"), P(("gx", "gy", "gz"), None, None)),
        check_vma=False,
    )
```

```python
import functools
import math

import jax
import jax.numpy as jnp
from jax import lax
from jax.experimental import pallas as pl
from jax.experimental.pallas import tpu as pltpu
from jax.sharding import PartitionSpec as P

MESH = pl.DeviceIdType.MESH
LANES = 128
ROWS = 8


def round_up(value, unit):
    return -(-value // unit) * unit


def iota(shape, dim):
    return lax.broadcasted_iota(jnp.int32, shape, dim)


def parts(value):
    high = value.astype(jnp.bfloat16)
    return high, (value - high.astype(jnp.float32)).astype(jnp.bfloat16)


def dot(left, right, dims):
    return lax.dot_general(left, right, (dims, ((), ())), preferred_element_type=jnp.float32)


NN = ((1,), (0,))
NT = ((1,), (1,))
TN = ((0,), (0,))


def flag(mask):
    return jnp.where(mask, 1.0, 0.0).astype(jnp.bfloat16)


def dot_three(left, right, dims):
    left_high, left_low = parts(left)
    right_high, right_low = parts(right)
    return (
        dot(left_high, right_high, dims)
        + dot(left_low, right_high, dims)
        + dot(left_high, right_low, dims)
    )


def kernel(
    sizes, source_ref, owner_ref, cell_ref, flow_any, courant_any, tracer_any,
    lambda_ref, wide_ref,
    flow_ref, courant_ref, tracer_ref, load_sem,
    payload_ref, well_send, well_recv, well_send_sem, well_recv_sem,
    rise_ref, fall_ref, sum_ref, grad_ref,
    x_send, x_recv, y_send, y_recv, z_send, z_recv, face_send_sem, face_recv_sem,
    carry_send, carry_recv, carry_send_sem, carry_recv_sem,
    enter_send, enter_recv, enter_send_sem, enter_recv_sem,
    bulk_send, bulk_recv, bulk_send_sem, bulk_recv_sem,
    table_high, table_low,
):
    n_gx, n_gy, n_gz, brick_z, brick_x, brick_y, cap = sizes
    steps = flow_any.shape[0]
    lines = brick_z * brick_x
    groups = n_gx * n_gy
    devices = groups * n_gz
    a, b, c = lax.axis_index("gx"), lax.axis_index("gy"), lax.axis_index("gz")
    group = a * n_gy + b
    me = group * n_gz + c
    wells = source_ref.shape[1]
    full_z = n_gz * brick_z
    full_x = n_gx * brick_x
    wide_x = round_up(full_x, LANES)
    shares = n_gx * n_gz
    y_rows = brick_y // shares
    pad_rows = round_up(y_rows, ROWS)
    tiles = lines // LANES
    tile_z = LANES // brick_x

    loads = [
        pltpu.make_async_copy(src, dst, load_sem.at[i])
        for i, (src, dst) in enumerate(
            ((courant_any, courant_ref), (flow_any, flow_ref), (tracer_any, tracer_ref))
        )
    ]
    for load in loads:
        load.start()

    for ref in (x_recv, y_recv, z_recv, carry_recv):
        ref[...] = jnp.zeros_like(ref)

    barrier = pltpu.get_barrier_semaphore()

    def greet(d, carried):
        other = lax.rem(me + d, devices)
        pl.semaphore_signal(
            barrier, inc=1,
            device_id=(
                lax.div(other, n_gy * n_gz), lax.rem(lax.div(other, n_gz), n_gy), lax.rem(other, n_gz)
            ),
            device_id_type=MESH,
        )
        return carried

    lax.fori_loop(1, devices, greet, 0)

    eye = iota((wells, wells), 0) == iota((wells, wells), 1)
    before = iota((wells, wells), 0) < iota((wells, wells), 1)
    owner_row = owner_ref[...].astype(jnp.float32)
    owner_col = jnp.sum(jnp.where(eye, owner_row, 0.0), axis=1, keepdims=True)
    rank_row = jnp.sum(
        jnp.where(before & (owner_col == owner_row), 1.0, 0.0), axis=0, keepdims=True
    )
    slots = groups * cap
    second = rank_row >= cap
    key_row = owner_row * cap + rank_row + jnp.where(second, slots - cap, 0)
    chosen = flag(iota((2 * slots, wells), 0) == key_row.astype(jnp.int32))
    cell_row = cell_ref[...]
    payload_ref[...] = jnp.zeros_like(payload_ref)
    payload_ref[0:brick_z, :] = source_ref[...]
    payload_ref[brick_z:brick_z + 1, :] = lax.div(cell_row, brick_y).astype(jnp.float32)
    payload_ref[brick_z + 1:brick_z + 2, :] = lax.rem(cell_row, brick_y).astype(jnp.float32)
    payload_high, payload_low = parts(payload_ref[...])
    sorted_wells = dot(chosen, payload_high, NT) + dot(chosen, payload_low, NT)
    well_send[...] = sorted_wells[0:slots] + pltpu.roll(sorted_wells[slots:], LANES // 2, 1)

    pl.semaphore_wait(barrier, devices - 1)

    def group_rows(index):
        return pl.ds(pl.multiple_of(index * cap, ROWS), cap)

    def well_copy(d):
        other = lax.rem(group + d, groups)
        return pltpu.make_async_remote_copy(
            src_ref=well_send.at[group_rows(other), :],
            dst_ref=well_recv.at[group_rows(group), :],
            send_sem=well_send_sem.at[d],
            recv_sem=well_recv_sem.at[d],
            device_id=(lax.div(other, n_gy), lax.rem(other, n_gy), c),
            device_id_type=MESH,
        )

    def well_start(d, carried):
        well_copy(d).start()
        return carried

    lax.fori_loop(1, groups, well_start, 0)
    well_recv[group_rows(group), :] = well_send[group_rows(group), :]

    shape = (n_gx * LANES, wide_x)
    at_x = lax.div(iota(shape, 0), LANES) * brick_x + lax.rem(iota(shape, 0), brick_x)
    far = jnp.abs(at_x - iota(shape, 1)).astype(jnp.float32)
    table = jnp.exp(far * (-0.5 / brick_x)) / math.sqrt(2 * brick_x) / math.sqrt(2 * brick_z)
    table = jnp.where(iota(shape, 1) < full_x, table, 0.0)
    depth_of = lax.rem(lax.div(iota(shape, 0), brick_x), tile_z)
    for depth in range(tile_z):
        high, low = parts(jnp.where(depth_of == depth, table, 0.0))
        table_high[:, depth * wide_x:(depth + 1) * wide_x] = high
        table_low[:, depth * wide_x:(depth + 1) * wide_x] = low

    spread = flag(lax.div(iota((lines, LANES), 0), brick_x) == iota((lines, LANES), 1))
    x_pick = flag(iota((ROWS, LANES), 1) == brick_z)

    loads[0].wait()
    loads[1].wait()
    loads[2].wait()

    def well_wait(d, carried):
        copy = well_copy(d)
        copy.wait_send()
        copy.wait_recv()
        return carried

    lax.fori_loop(1, groups, well_wait, 0)
    landed = well_recv[...]
    landed = jnp.concatenate([landed, pltpu.roll(landed, LANES // 2, 1)], axis=0)
    landed_high, landed_low = parts(landed)
    x_row = dot(x_pick, landed_high, NT)[0:1, :].astype(jnp.int32)
    x_hit = lax.rem(iota((lines, 2 * slots), 0), brick_x) == x_row
    y_hit = flag(
        iota((2 * slots, LANES), 1) == landed[:, brick_z + 1:brick_z + 2].astype(jnp.int32)
    )
    spread_high = jnp.where(x_hit, dot(spread, landed_high, NT), 0.0).astype(jnp.bfloat16)
    spread_low = jnp.where(x_hit, dot(spread, landed_low, NT), 0.0).astype(jnp.bfloat16)
    adjoint = dot(spread_high, y_hit, NN) + dot(spread_low, y_hit, NN)

    y_pos = iota((lines, brick_y), 1)
    x_pos = lax.rem(iota((lines, brick_y), 0), brick_x)
    take_row, take_lane = iota((2 * ROWS, brick_y), 0), iota((2 * ROWS, brick_y), 1)
    take = flag(
        ((take_row < ROWS) & (take_lane == 0)) | ((take_row >= ROWS) & (take_lane == brick_y - 1))
    )
    put = flag(
        ((take_row == 0) & (take_lane == brick_y - 1)) | ((take_row == ROWS) & (take_lane == 0))
    )

    def face_copies(step):
        copies = []
        for axis, (place, count, send, recv) in enumerate(
            ((a, n_gx, x_send, x_recv), (b, n_gy, y_send, y_recv), (c, n_gz, z_send, z_recv))
        ):
            for side in range(2):
                moved = place - 1 if side == 0 else place + 1
                target = [a, b, c]
                target[axis] = lax.rem(moved + count, count)
                sends = place > 0 if side == 0 else place < count - 1
                gets = place < count - 1 if side == 0 else place > 0
                copy = pltpu.make_async_remote_copy(
                    src_ref=send.at[step, side],
                    dst_ref=recv.at[step, side],
                    send_sem=face_send_sem.at[step, axis, side],
                    recv_sem=face_recv_sem.at[step, axis, side],
                    device_id=tuple(target),
                    device_id_type=MESH,
                )
                copies.append((copy, sends, gets))
        return copies

    def when_start(copy, sends):
        @pl.when(sends)
        def _():
            copy.start()

    all_copies = []
    for step in reversed(range(steps)):
        copies = face_copies(step)
        all_copies.extend(copies)
        flow = flow_ref[step]
        flows = [courant_ref[axis] * adjoint for axis in range(3)]
        rise = [
            jnp.where((flow & (1 << axis)) != 0, flows[axis], 0.0) for axis in range(3)
        ]
        fall = [flows[axis] - rise[axis] for axis in range(3)]
        z_send[step, 0] = rise[2][0:brick_x]
        z_send[step, 1] = fall[2][lines - brick_x:lines]
        when_start(*copies[4][:2])
        when_start(*copies[5][:2])
        rise_ref[...] = rise[0]
        fall_ref[...] = fall[0]
        x_send[step, 0] = rise_ref[pl.ds(0, brick_z, stride=brick_x), :]
        x_send[step, 1] = fall_ref[pl.ds(brick_x - 1, brick_z, stride=brick_x), :]
        when_start(*copies[0][:2])
        when_start(*copies[1][:2])
        edge = jnp.where(y_pos == 0, rise[1], jnp.where(y_pos == brick_y - 1, fall[1], 0.0))
        edge_high, edge_low = parts(edge)
        edge_rows = dot(take, edge_high, NT) + dot(take, edge_low, NT)
        y_send[step, 0] = edge_rows[0:ROWS]
        y_send[step, 1] = edge_rows[ROWS:2 * ROWS]
        when_start(*copies[2][:2])
        when_start(*copies[3][:2])

        rest = 1.0 - (courant_ref[0] + courant_ref[1] + courant_ref[2])
        updated = rest * adjoint
        updated = updated + jnp.where(
            x_pos == brick_x - 1, 0.0, pltpu.roll(rise[0], lines - 1, 0)
        )
        updated = updated + jnp.where(x_pos == 0, 0.0, pltpu.roll(fall[0], 1, 0))
        updated = updated + jnp.where(
            y_pos == brick_y - 1, 0.0, pltpu.roll(rise[1], brick_y - 1, 1)
        )
        updated = updated + jnp.where(y_pos == 0, 0.0, pltpu.roll(fall[1], 1, 1))
        border = jnp.zeros((brick_x, brick_y), jnp.float32)
        updated = updated + jnp.concatenate([rise[2][brick_x:], border], axis=0)
        updated = updated + jnp.concatenate([border, fall[2][:lines - brick_x]], axis=0)
        sum_ref[...] = updated

        for copy, _, gets in copies:
            @pl.when(gets)
            def _():
                copy.wait_recv()

        top = pl.ds(brick_x - 1, brick_z, stride=brick_x)
        bottom = pl.ds(0, brick_z, stride=brick_x)
        sum_ref[top, :] = sum_ref[top, :] + x_recv[step, 0]
        sum_ref[bottom, :] = sum_ref[bottom, :] + x_recv[step, 1]
        last = pl.ds(lines - brick_x, brick_x)
        sum_ref[last, :] = sum_ref[last, :] + z_recv[step, 0]
        first = pl.ds(0, brick_x)
        sum_ref[first, :] = sum_ref[first, :] + z_recv[step, 1]
        side_rows = jnp.concatenate([y_recv[step, 0], y_recv[step, 1]], axis=0)
        side_high, side_low = parts(side_rows)
        adjoint = sum_ref[...] + (dot(side_high, put, TN) + dot(side_low, put, TN))
        if step == steps - 1:
            gradient = adjoint * tracer_ref[step]
        else:
            gradient = grad_ref[...] + adjoint * tracer_ref[step]
        grad_ref[...] = gradient

    length = 2.0 * brick_y
    from_end = jnp.where(take_row < ROWS, brick_y - take_lane, take_lane + 1)
    pull = jnp.exp(from_end.astype(jnp.float32) * (-1.0 / length)) / math.sqrt(length)
    carries = dot_three(pull, gradient, NT)
    packed = [
        carries[row:row + 1, t * LANES:(t + 1) * LANES] for row in (0, ROWS) for t in range(tiles)
    ]
    carry_send[...] = jnp.concatenate(packed, axis=0)
    carry_copies = []
    for d in range(1, n_gy):
        for moved, back in ((b + d, b - d), (b - d, b + d)):
            copy = pltpu.make_async_remote_copy(
                src_ref=carry_send,
                dst_ref=carry_recv.at[b],
                send_sem=carry_send_sem.at[lax.rem(moved + n_gy, n_gy)],
                recv_sem=carry_recv_sem.at[b],
                device_id=(a, lax.rem(moved + n_gy, n_gy), c),
                device_id_type=MESH,
            )
            arrival = pltpu.make_async_remote_copy(
                src_ref=carry_send,
                dst_ref=carry_recv.at[lax.rem(back + n_gy, n_gy)],
                send_sem=carry_send_sem.at[lax.rem(back + n_gy, n_gy)],
                recv_sem=carry_recv_sem.at[lax.rem(back + n_gy, n_gy)],
                device_id=(a, lax.rem(moved + n_gy, n_gy), c),
                device_id_type=MESH,
            )
            sends = (moved >= 0) & (moved < n_gy)
            gets = (back >= 0) & (back < n_gy)
            when_start(copy, sends)
            carry_copies.append((copy, sends, arrival, gets))

    def line_place(row):
        return lax.div(row, pad_rows) * y_rows + lax.rem(row, pad_rows)

    shape = (shares * pad_rows, brick_y)
    near = jnp.abs(line_place(iota(shape, 0)) - iota(shape, 1)).astype(jnp.float32)
    table_y = jnp.exp(near * (-1.0 / length)) / math.sqrt(length)
    bulk_send[...] = dot_three(table_y, gradient, NT)

    mine = a * n_gz + c

    def bulk_copy(d):
        share = lax.rem(mine + d, shares)
        other = b * shares + share
        return other, pltpu.make_async_remote_copy(
            src_ref=bulk_send.at[pl.ds(pl.multiple_of(share * pad_rows, ROWS), pad_rows), :],
            dst_ref=bulk_recv.at[mine],
            send_sem=bulk_send_sem.at[share],
            recv_sem=bulk_recv_sem.at[mine],
            device_id=(
                lax.div(other, n_gy * n_gz), lax.rem(lax.div(other, n_gz), n_gy), lax.rem(other, n_gz)
            ),
            device_id_type=MESH,
        )

    def bulk_start(d, carried):
        other, copy = bulk_copy(d)

        @pl.when(other != me)
        def _():
            copy.start()

        return carried

    lax.fori_loop(0, shares, bulk_start, 0)
    lambda_ref[...] = adjoint

    own = lax.div(me, shares) == b

    @pl.when(own)
    def _():
        rows = pl.ds(pl.multiple_of((me - b * shares) * pad_rows, ROWS), pad_rows)
        bulk_recv[mine] = bulk_send[rows, :]

    for _, _, arrival, gets in carry_copies:
        @pl.when(gets)
        def _():
            arrival.wait_recv()

    carry_row = iota((2 * tiles, LANES), 0)
    entering = jnp.zeros((2 * tiles, LANES), jnp.float32)
    for brick in range(n_gy):
        between = jnp.where(carry_row < tiles, b - brick - 1, brick - b - 1)
        weight = jnp.exp(jnp.maximum(between, 0).astype(jnp.float32) * (-brick_y / length))
        entering = entering + jnp.where(between >= 0, weight, 0.0) * carry_recv[brick]
    enter_send[...] = entering

    def enter_copy(d):
        share = lax.rem(mine + d, shares)
        other = b * shares + share
        return other, pltpu.make_async_remote_copy(
            src_ref=enter_send,
            dst_ref=enter_recv.at[mine],
            send_sem=enter_send_sem.at[share],
            recv_sem=enter_recv_sem.at[mine],
            device_id=(
                lax.div(other, n_gy * n_gz), lax.rem(lax.div(other, n_gz), n_gy), lax.rem(other, n_gz)
            ),
            device_id_type=MESH,
        )

    def enter_start(d, carried):
        other, copy = enter_copy(d)

        @pl.when(other != me)
        def _():
            copy.start()

        return carried

    lax.fori_loop(0, shares, enter_start, 0)

    @pl.when(own)
    def _():
        enter_recv[mine] = enter_send[...]

    for copy, sends, _ in all_copies:
        @pl.when(sends)
        def _():
            copy.wait_send()

    for copy, sends, _, _ in carry_copies:
        @pl.when(sends)
        def _():
            copy.wait_send()

    at_y = lax.rem(me, shares) * y_rows + iota((pad_rows, LANES), 0)
    from_low = jnp.exp(at_y.astype(jnp.float32) * (-1.0 / length))
    from_high = jnp.exp(jnp.maximum(brick_y - 1 - at_y, 0).astype(jnp.float32) * (-1.0 / length))
    for i in range(n_gx):
        for k in range(n_gz):
            slot = i * n_gz + k

            @pl.when(jnp.logical_not(own & (mine == slot)))
            def _():
                for send, recv, send_sem, recv_sem in (
                    (bulk_send.at[pl.ds(0, pad_rows), :], bulk_recv, bulk_send_sem, bulk_recv_sem),
                    (enter_send, enter_recv, enter_send_sem, enter_recv_sem),
                ):
                    pltpu.make_async_remote_copy(
                        src_ref=send,
                        dst_ref=recv.at[slot],
                        send_sem=send_sem.at[slot],
                        recv_sem=recv_sem.at[slot],
                        device_id=(a, b, c),
                        device_id_type=MESH,
                    ).wait_recv()

        rows = []
        for k in range(n_gz):
            slot = i * n_gz + k
            for t in range(tiles):
                rows.append(
                    bulk_recv[slot, :, t * LANES:(t + 1) * LANES]
                    + from_low * enter_recv[slot, t:t + 1, :]
                    + from_high * enter_recv[slot, tiles + t:tiles + t + 1, :]
                )
        high, low = parts(jnp.concatenate(rows, axis=0))
        block_high = table_high[i * LANES:(i + 1) * LANES, :]
        block_low = table_low[i * LANES:(i + 1) * LANES, :]
        product = dot(high, block_high, NN) + dot(low, block_high, NN) + dot(high, block_low, NN)
        wide_ref[...] = product if i == 0 else wide_ref[...] + product

    def bulk_sent(d, carried):
        other, copy = bulk_copy(d)
        _, enter = enter_copy(d)

        @pl.when(other != me)
        def _():
            copy.wait_send()
            enter.wait_send()

        return carried

    lax.fori_loop(0, shares, bulk_sent, 0)


def depth_kernel(
    sizes, lambda_any, wide_ref, lambda_out, smooth_ref, copy_sem, stage_ref=None
):
    brick_z, full_z, full_x, y_rows, pad_rows, tile_z = sizes
    wide_x = round_up(full_x, LANES)
    copy = pltpu.make_async_copy(lambda_any, lambda_out, copy_sem)
    copy.start()

    fade = math.exp(-0.5 / brick_z)

    def plane(z):
        row, depth = z // tile_z * pad_rows, z % tile_z
        return wide_ref[row:row + y_rows, depth * wide_x:(depth + 1) * wide_x]

    ahead = [plane(0)]
    for z in range(1, full_z):
        ahead.append(plane(z) + fade * ahead[-1])
    behind = None
    for z in reversed(range(full_z)):
        total = ahead[z] if behind is None else ahead[z] + behind
        if full_x <= LANES:
            smooth_ref[pl.ds(z, y_rows, stride=full_z), :] = total[:, 0:full_x]
        else:
            for tile in range(wide_x // LANES):
                part = total[:, tile * LANES:(tile + 1) * LANES]
                stage_ref[tile, pl.ds(z, y_rows, stride=full_z), :] = part
        behind = fade * (plane(z) if behind is None else plane(z) + behind)

    if full_x > LANES:
        for tile in range(wide_x // LANES):
            end = min((tile + 1) * LANES, full_x)
            smooth_ref[:, tile * LANES:end] = stage_ref[tile][:, 0:end - tile * LANES]
    copy.wait()


def per_device(well_sources, well_owner, well_cell, flow_sign, courant, tracer):
    steps, brick_z, brick_x, brick_y = tracer.shape
    n_gx, n_gy, n_gz = lax.axis_size("gx"), lax.axis_size("gy"), lax.axis_size("gz")
    groups, shares = n_gx * n_gy, n_gx * n_gz
    wells = well_cell.shape[0]
    cap = round_up(-(-wells // groups), ROWS)
    lines = brick_z * brick_x
    y_rows = brick_y // shares
    pad_rows = round_up(y_rows, ROWS)
    full_x, full_z = n_gx * brick_x, n_gz * brick_z
    wide_x = round_up(full_x, LANES)
    tile_z = LANES // brick_x
    tiles = lines // LANES
    f32 = jnp.float32
    sizes = (n_gx, n_gy, n_gz, brick_z, brick_x, brick_y, cap)
    dma = pltpu.SemaphoreType.DMA
    vmem = pl.BlockSpec(memory_space=pltpu.VMEM)
    away = pl.BlockSpec(memory_space=pl.ANY)
    field = (3, lines, brick_y)
    stage = []
    if full_x > LANES:
        stage = [pltpu.VMEM((wide_x // LANES, y_rows * full_z, LANES), f32)]
    run = pl.pallas_call(
        functools.partial(kernel, sizes),
        out_shape=(
            jax.ShapeDtypeStruct((lines, brick_y), f32),
            jax.ShapeDtypeStruct((n_gz * tiles * pad_rows, tile_z * wide_x), f32),
        ),
        in_specs=[vmem, vmem, vmem, away, away, away],
        out_specs=(vmem, vmem),
        scratch_shapes=[
            pltpu.VMEM((steps, lines, brick_y), jnp.int32),
            pltpu.VMEM(field, f32),
            pltpu.VMEM((steps, lines, brick_y), f32),
            dma((3,)),
            pltpu.VMEM((LANES, wells), f32),
            pltpu.VMEM((groups * cap, LANES), f32),
            pltpu.VMEM((groups * cap, LANES), f32),
            dma((groups,)),
            dma((groups,)),
            pltpu.VMEM((lines, brick_y), f32),
            pltpu.VMEM((lines, brick_y), f32),
            pltpu.VMEM((lines, brick_y), f32),
            pltpu.VMEM((lines, brick_y), f32),
            pltpu.VMEM((steps, 2, brick_z, brick_y), f32),
            pltpu.VMEM((steps, 2, brick_z, brick_y), f32),
            pltpu.VMEM((steps, 2, ROWS, lines), f32),
            pltpu.VMEM((steps, 2, ROWS, lines), f32),
            pltpu.VMEM((steps, 2, brick_x, brick_y), f32),
            pltpu.VMEM((steps, 2, brick_x, brick_y), f32),
            dma((steps, 3, 2)),
            dma((steps, 3, 2)),
            pltpu.VMEM((2 * tiles, LANES), f32),
            pltpu.VMEM((n_gy, 2 * tiles, LANES), f32),
            dma((n_gy,)),
            dma((n_gy,)),
            pltpu.VMEM((2 * tiles, LANES), f32),
            pltpu.VMEM((shares, 2 * tiles, LANES), f32),
            dma((shares,)),
            dma((shares,)),
            pltpu.VMEM((shares * pad_rows, lines), f32),
            pltpu.VMEM((shares, pad_rows, lines), f32),
            dma((shares,)),
            dma((shares,)),
            pltpu.VMEM((n_gx * LANES, tile_z * wide_x), jnp.bfloat16),
            pltpu.VMEM((n_gx * LANES, tile_z * wide_x), jnp.bfloat16),
        ],
        compiler_params=pltpu.CompilerParams(
            collective_id=0, has_side_effects=True, vmem_limit_bytes=56 * 2**20
        ),
    )
    start, wide = run(
        well_sources.T,
        well_owner.reshape(1, wells),
        well_cell.reshape(1, wells),
        flow_sign.reshape(steps, lines, brick_y),
        courant.reshape(field),
        tracer.reshape(steps, lines, brick_y),
    )
    depth_sizes = (brick_z, full_z, full_x, y_rows, pad_rows, tile_z)
    start, smoothed = pl.pallas_call(
        functools.partial(depth_kernel, depth_sizes),
        out_shape=(
            jax.ShapeDtypeStruct((lines, brick_y), f32),
            jax.ShapeDtypeStruct((y_rows * full_z, full_x), f32),
        ),
        in_specs=[away, vmem],
        out_specs=(away, vmem),
        scratch_shapes=[dma] + stage,
    )(start, wide)
    return (
        start.reshape(brick_z, brick_x, brick_y),
        smoothed.reshape(y_rows, full_z, full_x),
    )


def solution(mesh):
    return jax.shard_map(
        per_device,
        mesh=mesh,
        in_specs=(
            P(("gx", "gy"), "gz"),
            P(("gx", "gy"), None),
            P(("gx", "gy")),
            P(None, "gz", "gx", "gy"),
            P(None, "gz", "gx", "gy"),
            P(None, "gz", "gx", "gy"),
        ),
        out_specs=(P("gz", "gx", "gy"), P(("gx", "gy", "gz"), None, None)),
        check_vma=False,
    )
```

```python
import functools
import math

import jax
import jax.numpy as jnp
from jax import lax
from jax.experimental import pallas as pl
from jax.experimental.pallas import tpu as pltpu
from jax.sharding import PartitionSpec as P

MESH = pl.DeviceIdType.MESH
LANES = 128
ROWS = 8


def round_up(value, unit):
    return -(-value // unit) * unit


def iota(shape, dim):
    return lax.broadcasted_iota(jnp.int32, shape, dim)


def parts(value):
    high = value.astype(jnp.bfloat16)
    return high, (value - high.astype(jnp.float32)).astype(jnp.bfloat16)


def dot(left, right, dims):
    return lax.dot_general(left, right, (dims, ((), ())), preferred_element_type=jnp.float32)


NN = ((1,), (0,))
NT = ((1,), (1,))
TN = ((0,), (0,))


def flag(mask):
    return jnp.where(mask, 1.0, 0.0).astype(jnp.bfloat16)


def dot_three(left, right, dims):
    left_high, left_low = parts(left)
    right_high, right_low = parts(right)
    return (
        dot(left_high, right_high, dims)
        + dot(left_low, right_high, dims)
        + dot(left_high, right_low, dims)
    )


def kernel(
    sizes, source_ref, owner_ref, cell_ref, flow_any, courant_any, tracer_any,
    lambda_ref, wide_ref,
    flow_ref, courant_ref, tracer_ref, load_sem,
    payload_ref, well_send, well_recv, well_send_sem, well_recv_sem,
    rise_ref, fall_ref, sum_ref, grad_ref,
    x_send, x_recv, y_send, y_recv, z_send, z_recv, face_send_sem, face_recv_sem,
    carry_send, carry_recv, carry_send_sem, carry_recv_sem,
    enter_send, enter_recv, enter_send_sem, enter_recv_sem,
    bulk_send, bulk_recv, bulk_send_sem, bulk_recv_sem,
    table_high, table_low,
):
    n_gx, n_gy, n_gz, brick_z, brick_x, brick_y, cap = sizes
    steps = flow_any.shape[0]
    lines = brick_z * brick_x
    groups = n_gx * n_gy
    devices = groups * n_gz
    a, b, c = lax.axis_index("gx"), lax.axis_index("gy"), lax.axis_index("gz")
    group = a * n_gy + b
    me = group * n_gz + c
    wells = source_ref.shape[1]
    full_z = n_gz * brick_z
    full_x = n_gx * brick_x
    wide_x = round_up(full_x, LANES)
    shares = n_gx * n_gz
    y_rows = brick_y // shares
    pad_rows = round_up(y_rows, ROWS)
    tiles = lines // LANES
    tile_z = LANES // brick_x

    courant_load = pltpu.make_async_copy(courant_any, courant_ref, load_sem.at[0, steps])
    courant_load.start()
    flow_loads, tracer_loads = (
        [
            pltpu.make_async_copy(src.at[step], dst.at[step], load_sem.at[kind, step])
            for step in range(steps)
        ]
        for kind, (src, dst) in enumerate(((flow_any, flow_ref), (tracer_any, tracer_ref)))
    )
    for step in reversed(range(steps)):
        flow_loads[step].start()
        tracer_loads[step].start()

    for ref in (x_recv, y_recv, z_recv, carry_recv):
        ref[...] = jnp.zeros_like(ref)

    barrier = pltpu.get_barrier_semaphore()

    def greet(d, carried):
        other = lax.rem(me + d, devices)
        pl.semaphore_signal(
            barrier, inc=1,
            device_id=(
                lax.div(other, n_gy * n_gz), lax.rem(lax.div(other, n_gz), n_gy), lax.rem(other, n_gz)
            ),
            device_id_type=MESH,
        )
        return carried

    lax.fori_loop(1, devices, greet, 0)

    eye = iota((wells, wells), 0) == iota((wells, wells), 1)
    before = iota((wells, wells), 0) < iota((wells, wells), 1)
    owner_row = owner_ref[...].astype(jnp.float32)
    owner_col = jnp.sum(jnp.where(eye, owner_row, 0.0), axis=1, keepdims=True)
    rank_row = jnp.sum(
        jnp.where(before & (owner_col == owner_row), 1.0, 0.0), axis=0, keepdims=True
    )
    slots = groups * cap
    second = rank_row >= cap
    key_row = owner_row * cap + rank_row + jnp.where(second, slots - cap, 0)
    chosen = flag(iota((2 * slots, wells), 0) == key_row.astype(jnp.int32))
    cell_row = cell_ref[...]
    payload_ref[...] = jnp.zeros_like(payload_ref)
    payload_ref[0:brick_z, :] = source_ref[...]
    payload_ref[brick_z:brick_z + 1, :] = lax.div(cell_row, brick_y).astype(jnp.float32)
    payload_ref[brick_z + 1:brick_z + 2, :] = lax.rem(cell_row, brick_y).astype(jnp.float32)
    payload_high, payload_low = parts(payload_ref[...])
    sorted_wells = dot(chosen, payload_high, NT) + dot(chosen, payload_low, NT)
    well_send[...] = sorted_wells[0:slots] + pltpu.roll(sorted_wells[slots:], LANES // 2, 1)

    pl.semaphore_wait(barrier, devices - 1)

    def group_rows(index):
        return pl.ds(pl.multiple_of(index * cap, ROWS), cap)

    def well_copy(d):
        other = lax.rem(group + d, groups)
        return pltpu.make_async_remote_copy(
            src_ref=well_send.at[group_rows(other), :],
            dst_ref=well_recv.at[group_rows(group), :],
            send_sem=well_send_sem.at[d],
            recv_sem=well_recv_sem.at[d],
            device_id=(lax.div(other, n_gy), lax.rem(other, n_gy), c),
            device_id_type=MESH,
        )

    def well_start(d, carried):
        well_copy(d).start()
        return carried

    lax.fori_loop(1, groups, well_start, 0)
    well_recv[group_rows(group), :] = well_send[group_rows(group), :]

    shape = (n_gx * LANES, wide_x)
    at_x = lax.div(iota(shape, 0), LANES) * brick_x + lax.rem(iota(shape, 0), brick_x)
    far = jnp.abs(at_x - iota(shape, 1)).astype(jnp.float32)
    table = jnp.exp(far * (-0.5 / brick_x)) / math.sqrt(2 * brick_x) / math.sqrt(2 * brick_z)
    table = jnp.where(iota(shape, 1) < full_x, table, 0.0)
    depth_of = lax.rem(lax.div(iota(shape, 0), brick_x), tile_z)
    for depth in range(tile_z):
        high, low = parts(jnp.where(depth_of == depth, table, 0.0))
        table_high[:, depth * wide_x:(depth + 1) * wide_x] = high
        table_low[:, depth * wide_x:(depth + 1) * wide_x] = low

    spread = flag(lax.div(iota((lines, LANES), 0), brick_x) == iota((lines, LANES), 1))
    x_pick = flag(iota((ROWS, LANES), 1) == brick_z)

    courant_load.wait()

    def well_wait(d, carried):
        well_copy(d).wait_recv()
        return carried

    def well_sent(d, carried):
        well_copy(d).wait_send()
        return carried

    lax.fori_loop(1, groups, well_wait, 0)
    landed = well_recv[...]
    landed = jnp.concatenate([landed, pltpu.roll(landed, LANES // 2, 1)], axis=0)
    landed_high, landed_low = parts(landed)
    x_row = dot(x_pick, landed_high, NT)[0:1, :].astype(jnp.int32)
    x_hit = lax.rem(iota((lines, 2 * slots), 0), brick_x) == x_row
    y_hit = flag(
        iota((2 * slots, LANES), 1) == landed[:, brick_z + 1:brick_z + 2].astype(jnp.int32)
    )
    spread_high = jnp.where(x_hit, dot(spread, landed_high, NT), 0.0).astype(jnp.bfloat16)
    spread_low = jnp.where(x_hit, dot(spread, landed_low, NT), 0.0).astype(jnp.bfloat16)
    adjoint = dot(spread_high, y_hit, NN) + dot(spread_low, y_hit, NN)

    y_pos = iota((lines, brick_y), 1)
    x_pos = lax.rem(iota((lines, brick_y), 0), brick_x)
    take_row, take_lane = iota((2 * ROWS, brick_y), 0), iota((2 * ROWS, brick_y), 1)
    take = flag(
        ((take_row < ROWS) & (take_lane == 0)) | ((take_row >= ROWS) & (take_lane == brick_y - 1))
    )
    put = flag(
        ((take_row == 0) & (take_lane == brick_y - 1)) | ((take_row == ROWS) & (take_lane == 0))
    )

    def face_copies(step):
        copies = []
        for axis, (place, count, send, recv) in enumerate(
            ((a, n_gx, x_send, x_recv), (b, n_gy, y_send, y_recv), (c, n_gz, z_send, z_recv))
        ):
            for side in range(2):
                moved = place - 1 if side == 0 else place + 1
                target = [a, b, c]
                target[axis] = lax.rem(moved + count, count)
                sends = place > 0 if side == 0 else place < count - 1
                gets = place < count - 1 if side == 0 else place > 0
                copy = pltpu.make_async_remote_copy(
                    src_ref=send.at[step, side],
                    dst_ref=recv.at[step, side],
                    send_sem=face_send_sem.at[step, axis, side],
                    recv_sem=face_recv_sem.at[step, axis, side],
                    device_id=tuple(target),
                    device_id_type=MESH,
                )
                copies.append((copy, sends, gets))
        return copies

    def when_start(copy, sends):
        @pl.when(sends)
        def _():
            copy.start()

    all_copies = []
    for step in reversed(range(steps)):
        copies = face_copies(step)
        all_copies.extend(copies)
        flow_loads[step].wait()
        flow = flow_ref[step]
        flows = [courant_ref[axis] * adjoint for axis in range(3)]
        rise = [
            jnp.where((flow & (1 << axis)) != 0, flows[axis], 0.0) for axis in range(3)
        ]
        fall = [flows[axis] - rise[axis] for axis in range(3)]
        z_send[step, 0] = rise[2][0:brick_x]
        z_send[step, 1] = fall[2][lines - brick_x:lines]
        when_start(*copies[4][:2])
        when_start(*copies[5][:2])
        rise_ref[...] = rise[0]
        fall_ref[...] = fall[0]
        x_send[step, 0] = rise_ref[pl.ds(0, brick_z, stride=brick_x), :]
        x_send[step, 1] = fall_ref[pl.ds(brick_x - 1, brick_z, stride=brick_x), :]
        when_start(*copies[0][:2])
        when_start(*copies[1][:2])
        edge = jnp.where(y_pos == 0, rise[1], jnp.where(y_pos == brick_y - 1, fall[1], 0.0))
        edge_high, edge_low = parts(edge)
        edge_rows = dot(take, edge_high, NT) + dot(take, edge_low, NT)
        y_send[step, 0] = edge_rows[0:ROWS]
        y_send[step, 1] = edge_rows[ROWS:2 * ROWS]
        when_start(*copies[2][:2])
        when_start(*copies[3][:2])

        rest = 1.0 - (courant_ref[0] + courant_ref[1] + courant_ref[2])
        updated = rest * adjoint
        updated = updated + jnp.where(
            x_pos == brick_x - 1, 0.0, pltpu.roll(rise[0], lines - 1, 0)
        )
        updated = updated + jnp.where(x_pos == 0, 0.0, pltpu.roll(fall[0], 1, 0))
        updated = updated + jnp.where(
            y_pos == brick_y - 1, 0.0, pltpu.roll(rise[1], brick_y - 1, 1)
        )
        updated = updated + jnp.where(y_pos == 0, 0.0, pltpu.roll(fall[1], 1, 1))
        border = jnp.zeros((brick_x, brick_y), jnp.float32)
        updated = updated + jnp.concatenate([rise[2][brick_x:], border], axis=0)
        updated = updated + jnp.concatenate([border, fall[2][:lines - brick_x]], axis=0)
        sum_ref[...] = updated

        for copy, _, gets in copies:
            @pl.when(gets)
            def _():
                copy.wait_recv()

        top = pl.ds(brick_x - 1, brick_z, stride=brick_x)
        bottom = pl.ds(0, brick_z, stride=brick_x)
        sum_ref[top, :] = sum_ref[top, :] + x_recv[step, 0]
        sum_ref[bottom, :] = sum_ref[bottom, :] + x_recv[step, 1]
        last = pl.ds(lines - brick_x, brick_x)
        sum_ref[last, :] = sum_ref[last, :] + z_recv[step, 0]
        first = pl.ds(0, brick_x)
        sum_ref[first, :] = sum_ref[first, :] + z_recv[step, 1]
        side_rows = jnp.concatenate([y_recv[step, 0], y_recv[step, 1]], axis=0)
        side_high, side_low = parts(side_rows)
        adjoint = sum_ref[...] + (dot(side_high, put, TN) + dot(side_low, put, TN))
        tracer_loads[step].wait()
        if step == steps - 1:
            gradient = adjoint * tracer_ref[step]
        else:
            gradient = grad_ref[...] + adjoint * tracer_ref[step]
        grad_ref[...] = gradient

    length = 2.0 * brick_y
    from_end = jnp.where(take_row < ROWS, brick_y - take_lane, take_lane + 1)
    pull = jnp.exp(from_end.astype(jnp.float32) * (-1.0 / length)) / math.sqrt(length)
    carries = dot_three(pull, gradient, NT)
    packed = [
        carries[row:row + 1, t * LANES:(t + 1) * LANES] for row in (0, ROWS) for t in range(tiles)
    ]
    carry_send[...] = jnp.concatenate(packed, axis=0)
    carry_copies = []
    for d in range(1, n_gy):
        for moved, back in ((b + d, b - d), (b - d, b + d)):
            copy = pltpu.make_async_remote_copy(
                src_ref=carry_send,
                dst_ref=carry_recv.at[b],
                send_sem=carry_send_sem.at[lax.rem(moved + n_gy, n_gy)],
                recv_sem=carry_recv_sem.at[b],
                device_id=(a, lax.rem(moved + n_gy, n_gy), c),
                device_id_type=MESH,
            )
            arrival = pltpu.make_async_remote_copy(
                src_ref=carry_send,
                dst_ref=carry_recv.at[lax.rem(back + n_gy, n_gy)],
                send_sem=carry_send_sem.at[lax.rem(back + n_gy, n_gy)],
                recv_sem=carry_recv_sem.at[lax.rem(back + n_gy, n_gy)],
                device_id=(a, lax.rem(moved + n_gy, n_gy), c),
                device_id_type=MESH,
            )
            sends = (moved >= 0) & (moved < n_gy)
            gets = (back >= 0) & (back < n_gy)
            when_start(copy, sends)
            carry_copies.append((copy, sends, arrival, gets))

    def line_place(row):
        return lax.div(row, pad_rows) * y_rows + lax.rem(row, pad_rows)

    shape = (shares * pad_rows, brick_y)
    near = jnp.abs(line_place(iota(shape, 0)) - iota(shape, 1)).astype(jnp.float32)
    table_y = jnp.exp(near * (-1.0 / length)) / math.sqrt(length)
    bulk_send[...] = dot_three(table_y, gradient, NT)

    mine = a * n_gz + c

    def bulk_copy(d):
        share = lax.rem(mine + d, shares)
        other = b * shares + share
        return other, pltpu.make_async_remote_copy(
            src_ref=bulk_send.at[pl.ds(pl.multiple_of(share * pad_rows, ROWS), pad_rows), :],
            dst_ref=bulk_recv.at[mine],
            send_sem=bulk_send_sem.at[share],
            recv_sem=bulk_recv_sem.at[mine],
            device_id=(
                lax.div(other, n_gy * n_gz), lax.rem(lax.div(other, n_gz), n_gy), lax.rem(other, n_gz)
            ),
            device_id_type=MESH,
        )

    def bulk_start(d, carried):
        other, copy = bulk_copy(d)

        @pl.when(other != me)
        def _():
            copy.start()

        return carried

    lax.fori_loop(0, shares, bulk_start, 0)
    lambda_ref[...] = adjoint

    own = lax.div(me, shares) == b

    @pl.when(own)
    def _():
        rows = pl.ds(pl.multiple_of((me - b * shares) * pad_rows, ROWS), pad_rows)
        bulk_recv[mine] = bulk_send[rows, :]

    for _, _, arrival, gets in carry_copies:
        @pl.when(gets)
        def _():
            arrival.wait_recv()

    carry_row = iota((2 * tiles, LANES), 0)
    entering = jnp.zeros((2 * tiles, LANES), jnp.float32)
    for brick in range(n_gy):
        between = jnp.where(carry_row < tiles, b - brick - 1, brick - b - 1)
        weight = jnp.exp(jnp.maximum(between, 0).astype(jnp.float32) * (-brick_y / length))
        entering = entering + jnp.where(between >= 0, weight, 0.0) * carry_recv[brick]
    enter_send[...] = entering

    def enter_copy(d):
        share = lax.rem(mine + d, shares)
        other = b * shares + share
        return other, pltpu.make_async_remote_copy(
            src_ref=enter_send,
            dst_ref=enter_recv.at[mine],
            send_sem=enter_send_sem.at[share],
            recv_sem=enter_recv_sem.at[mine],
            device_id=(
                lax.div(other, n_gy * n_gz), lax.rem(lax.div(other, n_gz), n_gy), lax.rem(other, n_gz)
            ),
            device_id_type=MESH,
        )

    def enter_start(d, carried):
        other, copy = enter_copy(d)

        @pl.when(other != me)
        def _():
            copy.start()

        return carried

    lax.fori_loop(0, shares, enter_start, 0)

    @pl.when(own)
    def _():
        enter_recv[mine] = enter_send[...]

    for copy, sends, _ in all_copies:
        @pl.when(sends)
        def _():
            copy.wait_send()

    for copy, sends, _, _ in carry_copies:
        @pl.when(sends)
        def _():
            copy.wait_send()

    at_y = lax.rem(me, shares) * y_rows + iota((pad_rows, LANES), 0)
    from_low = jnp.exp(at_y.astype(jnp.float32) * (-1.0 / length))
    from_high = jnp.exp(jnp.maximum(brick_y - 1 - at_y, 0).astype(jnp.float32) * (-1.0 / length))
    for i in range(n_gx):
        for k in range(n_gz):
            slot = i * n_gz + k

            @pl.when(jnp.logical_not(own & (mine == slot)))
            def _():
                for send, recv, send_sem, recv_sem in (
                    (bulk_send.at[pl.ds(0, pad_rows), :], bulk_recv, bulk_send_sem, bulk_recv_sem),
                    (enter_send, enter_recv, enter_send_sem, enter_recv_sem),
                ):
                    pltpu.make_async_remote_copy(
                        src_ref=send,
                        dst_ref=recv.at[slot],
                        send_sem=send_sem.at[slot],
                        recv_sem=recv_sem.at[slot],
                        device_id=(a, b, c),
                        device_id_type=MESH,
                    ).wait_recv()

        rows = []
        for k in range(n_gz):
            slot = i * n_gz + k
            for t in range(tiles):
                rows.append(
                    bulk_recv[slot, :, t * LANES:(t + 1) * LANES]
                    + from_low * enter_recv[slot, t:t + 1, :]
                    + from_high * enter_recv[slot, tiles + t:tiles + t + 1, :]
                )
        high, low = parts(jnp.concatenate(rows, axis=0))
        block_high = table_high[i * LANES:(i + 1) * LANES, :]
        block_low = table_low[i * LANES:(i + 1) * LANES, :]
        product = dot(high, block_high, NN) + dot(low, block_high, NN) + dot(high, block_low, NN)
        wide_ref[...] = product if i == 0 else wide_ref[...] + product

    def bulk_sent(d, carried):
        other, copy = bulk_copy(d)
        _, enter = enter_copy(d)

        @pl.when(other != me)
        def _():
            copy.wait_send()
            enter.wait_send()

        return carried

    lax.fori_loop(0, shares, bulk_sent, 0)
    lax.fori_loop(1, groups, well_sent, 0)


def depth_kernel(
    sizes, lambda_ref, wide_ref, lambda_out, smooth_ref, stage_ref=None
):
    brick_z, full_z, full_x, y_rows, pad_rows, tile_z = sizes
    wide_x = round_up(full_x, LANES)
    lambda_out[...] = lambda_ref[...]

    fade = math.exp(-0.5 / brick_z)

    def plane(z):
        row, depth = z // tile_z * pad_rows, z % tile_z
        return wide_ref[row:row + y_rows, depth * wide_x:(depth + 1) * wide_x]

    ahead = [plane(0)]
    for z in range(1, full_z):
        ahead.append(plane(z) + fade * ahead[-1])
    behind = None
    for z in reversed(range(full_z)):
        total = ahead[z] if behind is None else ahead[z] + behind
        if full_x <= LANES:
            smooth_ref[pl.ds(z, y_rows, stride=full_z), :] = total[:, 0:full_x]
        else:
            for tile in range(wide_x // LANES):
                part = total[:, tile * LANES:(tile + 1) * LANES]
                stage_ref[tile, pl.ds(z, y_rows, stride=full_z), :] = part
        behind = fade * (plane(z) if behind is None else plane(z) + behind)

    if full_x > LANES:
        for tile in range(wide_x // LANES):
            end = min((tile + 1) * LANES, full_x)
            smooth_ref[:, tile * LANES:end] = stage_ref[tile][:, 0:end - tile * LANES]


def per_device(well_sources, well_owner, well_cell, flow_sign, courant, tracer):
    steps, brick_z, brick_x, brick_y = tracer.shape
    n_gx, n_gy, n_gz = lax.axis_size("gx"), lax.axis_size("gy"), lax.axis_size("gz")
    groups, shares = n_gx * n_gy, n_gx * n_gz
    wells = well_cell.shape[0]
    cap = round_up(-(-wells // groups), ROWS)
    lines = brick_z * brick_x
    y_rows = brick_y // shares
    pad_rows = round_up(y_rows, ROWS)
    full_x, full_z = n_gx * brick_x, n_gz * brick_z
    wide_x = round_up(full_x, LANES)
    tile_z = LANES // brick_x
    tiles = lines // LANES
    f32 = jnp.float32
    sizes = (n_gx, n_gy, n_gz, brick_z, brick_x, brick_y, cap)
    dma = pltpu.SemaphoreType.DMA
    vmem = pl.BlockSpec(memory_space=pltpu.VMEM)
    away = pl.BlockSpec(memory_space=pl.ANY)
    field = (3, lines, brick_y)
    stage = []
    if full_x > LANES:
        stage = [pltpu.VMEM((wide_x // LANES, y_rows * full_z, LANES), f32)]
    run = pl.pallas_call(
        functools.partial(kernel, sizes),
        out_shape=(
            jax.ShapeDtypeStruct((lines, brick_y), f32),
            jax.ShapeDtypeStruct((n_gz * tiles * pad_rows, tile_z * wide_x), f32),
        ),
        in_specs=[vmem, vmem, vmem, away, away, away],
        out_specs=(vmem, vmem),
        scratch_shapes=[
            pltpu.VMEM((steps, lines, brick_y), jnp.int32),
            pltpu.VMEM(field, f32),
            pltpu.VMEM((steps, lines, brick_y), f32),
            dma((2, steps + 1)),
            pltpu.VMEM((LANES, wells), f32),
            pltpu.VMEM((groups * cap, LANES), f32),
            pltpu.VMEM((groups * cap, LANES), f32),
            dma((groups,)),
            dma((groups,)),
            pltpu.VMEM((lines, brick_y), f32),
            pltpu.VMEM((lines, brick_y), f32),
            pltpu.VMEM((lines, brick_y), f32),
            pltpu.VMEM((lines, brick_y), f32),
            pltpu.VMEM((steps, 2, brick_z, brick_y), f32),
            pltpu.VMEM((steps, 2, brick_z, brick_y), f32),
            pltpu.VMEM((steps, 2, ROWS, lines), f32),
            pltpu.VMEM((steps, 2, ROWS, lines), f32),
            pltpu.VMEM((steps, 2, brick_x, brick_y), f32),
            pltpu.VMEM((steps, 2, brick_x, brick_y), f32),
            dma((steps, 3, 2)),
            dma((steps, 3, 2)),
            pltpu.VMEM((2 * tiles, LANES), f32),
            pltpu.VMEM((n_gy, 2 * tiles, LANES), f32),
            dma((n_gy,)),
            dma((n_gy,)),
            pltpu.VMEM((2 * tiles, LANES), f32),
            pltpu.VMEM((shares, 2 * tiles, LANES), f32),
            dma((shares,)),
            dma((shares,)),
            pltpu.VMEM((shares * pad_rows, lines), f32),
            pltpu.VMEM((shares, pad_rows, lines), f32),
            dma((shares,)),
            dma((shares,)),
            pltpu.VMEM((n_gx * LANES, tile_z * wide_x), jnp.bfloat16),
            pltpu.VMEM((n_gx * LANES, tile_z * wide_x), jnp.bfloat16),
        ],
        compiler_params=pltpu.CompilerParams(
            collective_id=0, has_side_effects=True, vmem_limit_bytes=56 * 2**20
        ),
    )
    start, wide = run(
        well_sources.T,
        well_owner.reshape(1, wells),
        well_cell.reshape(1, wells),
        flow_sign.reshape(steps, lines, brick_y),
        courant.reshape(field),
        tracer.reshape(steps, lines, brick_y),
    )
    depth_sizes = (brick_z, full_z, full_x, y_rows, pad_rows, tile_z)
    start, smoothed = pl.pallas_call(
        functools.partial(depth_kernel, depth_sizes),
        out_shape=(
            jax.ShapeDtypeStruct((lines, brick_y), f32),
            jax.ShapeDtypeStruct((y_rows * full_z, full_x), f32),
        ),
        in_specs=[vmem, vmem],
        out_specs=(vmem, vmem),
        scratch_shapes=stage,
    )(start, wide)
    return (
        start.reshape(brick_z, brick_x, brick_y),
        smoothed.reshape(y_rows, full_z, full_x),
    )


def solution(mesh):
    return jax.shard_map(
        per_device,
        mesh=mesh,
        in_specs=(
            P(("gx", "gy"), "gz"),
            P(("gx", "gy"), None),
            P(("gx", "gy")),
            P(None, "gz", "gx", "gy"),
            P(None, "gz", "gx", "gy"),
            P(None, "gz", "gx", "gy"),
        ),
        out_specs=(P("gz", "gx", "gy"), P(("gx", "gy", "gz"), None, None)),
        check_vma=False,
    )
```

```python
import functools
import math

import jax
import jax.numpy as jnp
from jax import lax
from jax.experimental import pallas as pl
from jax.experimental.pallas import tpu as pltpu
from jax.sharding import PartitionSpec as P

MESH = pl.DeviceIdType.MESH
LANES = 128
ROWS = 8


def round_up(value, unit):
    return -(-value // unit) * unit


def iota(shape, dim):
    return lax.broadcasted_iota(jnp.int32, shape, dim)


def div(value, by):
    return value >> (by.bit_length() - 1) if by & (by - 1) == 0 else lax.div(value, by)


def rem(value, by):
    return value & (by - 1) if by & (by - 1) == 0 else lax.rem(value, by)


def each(start, stop, act):
    if stop - start <= 32:
        for i in range(start, stop):
            act(i)
    else:
        lax.fori_loop(start, stop, lambda i, carried: (act(i), carried)[1], 0)


def parts(value):
    high = value.astype(jnp.bfloat16)
    return high, (value - high.astype(jnp.float32)).astype(jnp.bfloat16)


def dot(left, right, dims):
    return lax.dot_general(left, right, (dims, ((), ())), preferred_element_type=jnp.float32)


NN = ((1,), (0,))
NT = ((1,), (1,))
TN = ((0,), (0,))


def flag(mask):
    return jnp.where(mask, 1.0, 0.0).astype(jnp.bfloat16)


def dot_three(left, right, dims):
    left_high, left_low = parts(left)
    right_high, right_low = parts(right)
    return (
        dot(left_high, right_high, dims)
        + dot(left_low, right_high, dims)
        + dot(left_high, right_low, dims)
    )


def kernel(
    sizes, source_any, owner_any, cell_any, flow_any, courant_any, tracer_any,
    lambda_any, wide_ref, lambda_ref, lambda_sem,
    source_ref, owner_ref, cell_ref, small_sem,
    flow_ref, courant_ref, tracer_ref, load_sem,
    payload_ref, well_send, well_recv, well_send_sem, well_recv_sem,
    rise_ref, fall_ref, sum_ref, grad_ref,
    x_send, x_recv, y_send, y_recv, z_send, z_recv, face_send_sem, face_recv_sem,
    carry_send, carry_recv, carry_send_sem, carry_recv_sem,
    enter_send, enter_recv, enter_send_sem, enter_recv_sem,
    bulk_send, bulk_recv, bulk_send_sem, bulk_recv_sem,
    table_high, table_low, y_high, y_low,
):
    n_gx, n_gy, n_gz, brick_z, brick_x, brick_y, cap = sizes
    steps = flow_any.shape[0]
    length = 2.0 * brick_y
    lines = brick_z * brick_x
    groups = n_gx * n_gy
    devices = groups * n_gz
    a, b, c = lax.axis_index("gx"), lax.axis_index("gy"), lax.axis_index("gz")
    group = a * n_gy + b
    me = group * n_gz + c
    wells = source_any.shape[1]
    full_z = n_gz * brick_z
    full_x = n_gx * brick_x
    wide_x = round_up(full_x, LANES)
    shares = n_gx * n_gz
    y_rows = brick_y // shares
    pad_rows = round_up(y_rows, ROWS)
    tiles = lines // LANES
    tile_z = LANES // brick_x

    for ref in (x_recv, y_recv, z_recv, carry_recv):
        ref[...] = jnp.zeros_like(ref)

    barrier = pltpu.get_barrier_semaphore()

    def greet(d):
        other = rem(me + d, devices)
        pl.semaphore_signal(
            barrier, inc=1,
            device_id=(
                div(other, n_gy * n_gz), rem(div(other, n_gz), n_gy), rem(other, n_gz)
            ),
            device_id_type=MESH,
        )

    each(1, devices, greet)
    small_loads = [
        pltpu.make_async_copy(src, dst, small_sem.at[i])
        for i, (src, dst) in enumerate(
            ((owner_any, owner_ref), (cell_any, cell_ref), (source_any, source_ref))
        )
    ]
    for load in small_loads:
        load.start()
    courant_load = pltpu.make_async_copy(courant_any, courant_ref, load_sem.at[0, steps])
    courant_load.start()
    flow_loads, tracer_loads = (
        [
            pltpu.make_async_copy(src.at[step], dst.at[step], load_sem.at[kind, step])
            for step in range(steps)
        ]
        for kind, (src, dst) in enumerate(((flow_any, flow_ref), (tracer_any, tracer_ref)))
    )
    for step in reversed(range(steps)):
        flow_loads[step].start()
        tracer_loads[step].start()

    eye = iota((wells, wells), 0) == iota((wells, wells), 1)
    before = iota((wells, wells), 0) < iota((wells, wells), 1)
    for load in small_loads:
        load.wait()
    owner_row = owner_ref[...].astype(jnp.float32)
    owner_col = jnp.sum(jnp.where(eye, owner_row, 0.0), axis=1, keepdims=True)
    rank_row = jnp.sum(
        jnp.where(before & (owner_col == owner_row), 1.0, 0.0), axis=0, keepdims=True
    )
    slots = groups * cap
    second = rank_row >= cap
    key_row = owner_row * cap + rank_row + jnp.where(second, slots - cap, 0)
    chosen = flag(iota((2 * slots, wells), 0) == key_row.astype(jnp.int32))
    cell_row = cell_ref[...]
    payload_ref[...] = jnp.zeros_like(payload_ref)
    payload_ref[0:brick_z, :] = source_ref[...]
    payload_ref[brick_z:brick_z + 1, :] = div(cell_row, brick_y).astype(jnp.float32)
    payload_ref[brick_z + 1:brick_z + 2, :] = rem(cell_row, brick_y).astype(jnp.float32)
    payload_high, payload_low = parts(payload_ref[...])
    sorted_wells = dot(chosen, payload_high, NT) + dot(chosen, payload_low, NT)
    well_send[...] = sorted_wells[0:slots] + pltpu.roll(sorted_wells[slots:], LANES // 2, 1)

    pl.semaphore_wait(barrier, devices - 1)

    def group_rows(index):
        return pl.ds(pl.multiple_of(index * cap, ROWS), cap)

    def well_copy(d):
        other = rem(group + d, groups)
        return pltpu.make_async_remote_copy(
            src_ref=well_send.at[group_rows(other), :],
            dst_ref=well_recv.at[group_rows(group), :],
            send_sem=well_send_sem.at[d],
            recv_sem=well_recv_sem.at[d],
            device_id=(div(other, n_gy), rem(other, n_gy), c),
            device_id_type=MESH,
        )

    def well_start(d):
        well_copy(d).start()

    each(1, groups, well_start)
    well_recv[group_rows(group), :] = well_send[group_rows(group), :]

    shape = (n_gx * LANES, wide_x)
    at_x = div(iota(shape, 0), LANES) * brick_x + rem(iota(shape, 0), brick_x)
    far = jnp.abs(at_x - iota(shape, 1)).astype(jnp.float32)
    table = jnp.exp(far * (-0.5 / brick_x)) / math.sqrt(2 * brick_x) / math.sqrt(2 * brick_z)
    table = jnp.where(iota(shape, 1) < full_x, table, 0.0)
    depth_of = rem(div(iota(shape, 0), brick_x), tile_z)
    for depth in range(tile_z):
        high, low = parts(jnp.where(depth_of == depth, table, 0.0))
        table_high[:, depth * wide_x:(depth + 1) * wide_x] = high
        table_low[:, depth * wide_x:(depth + 1) * wide_x] = low

    def line_place(row):
        return div(row, pad_rows) * y_rows + rem(row, pad_rows)

    shape = (shares * pad_rows, brick_y)
    near = jnp.abs(line_place(iota(shape, 0)) - iota(shape, 1)).astype(jnp.float32)
    table_y = jnp.exp(near * (-1.0 / length)) / math.sqrt(length)
    y_high[...], y_low[...] = parts(table_y)

    spread = flag(div(iota((lines, LANES), 0), brick_x) == iota((lines, LANES), 1))
    x_pick = flag(iota((ROWS, LANES), 1) == brick_z)

    courant_load.wait()

    def well_wait(d):
        well_copy(d).wait_recv()

    def well_sent(d):
        well_copy(d).wait_send()

    each(1, groups, well_wait)
    landed = well_recv[...]
    landed = jnp.concatenate([landed, pltpu.roll(landed, LANES // 2, 1)], axis=0)
    landed_high, landed_low = parts(landed)
    x_row = dot(x_pick, landed_high, NT)[0:1, :].astype(jnp.int32)
    x_hit = rem(iota((lines, 2 * slots), 0), brick_x) == x_row
    y_hit = flag(
        iota((2 * slots, LANES), 1) == landed[:, brick_z + 1:brick_z + 2].astype(jnp.int32)
    )
    spread_high = jnp.where(x_hit, dot(spread, landed_high, NT), 0.0).astype(jnp.bfloat16)
    spread_low = jnp.where(x_hit, dot(spread, landed_low, NT), 0.0).astype(jnp.bfloat16)
    adjoint = dot(spread_high, y_hit, NN) + dot(spread_low, y_hit, NN)

    y_pos = iota((lines, brick_y), 1)
    x_pos = rem(iota((lines, brick_y), 0), brick_x)
    take_row, take_lane = iota((2 * ROWS, brick_y), 0), iota((2 * ROWS, brick_y), 1)
    take = flag(
        ((take_row < ROWS) & (take_lane == 0)) | ((take_row >= ROWS) & (take_lane == brick_y - 1))
    )
    put = flag(
        ((take_row == 0) & (take_lane == brick_y - 1)) | ((take_row == ROWS) & (take_lane == 0))
    )

    def face_copies(step):
        copies = []
        for axis, (place, count, send, recv) in enumerate(
            ((a, n_gx, x_send, x_recv), (b, n_gy, y_send, y_recv), (c, n_gz, z_send, z_recv))
        ):
            for side in range(2):
                moved = place - 1 if side == 0 else place + 1
                target = [a, b, c]
                target[axis] = rem(moved + count, count)
                sends = place > 0 if side == 0 else place < count - 1
                gets = place < count - 1 if side == 0 else place > 0
                copy = pltpu.make_async_remote_copy(
                    src_ref=send.at[step, side],
                    dst_ref=recv.at[step, side],
                    send_sem=face_send_sem.at[step, axis, side],
                    recv_sem=face_recv_sem.at[step, axis, side],
                    device_id=tuple(target),
                    device_id_type=MESH,
                )
                copies.append((copy, sends, gets))
        return copies

    def when_start(copy, sends):
        @pl.when(sends)
        def _():
            copy.start()

    all_copies = []
    for step in reversed(range(steps)):
        copies = face_copies(step)
        all_copies.extend(copies)
        flow_loads[step].wait()
        flow = flow_ref[step]
        flows = [courant_ref[axis] * adjoint for axis in range(3)]
        rise = [
            jnp.where((flow & (1 << axis)) != 0, flows[axis], 0.0) for axis in range(3)
        ]
        fall = [flows[axis] - rise[axis] for axis in range(3)]
        z_send[step, 0] = rise[2][0:brick_x]
        z_send[step, 1] = fall[2][lines - brick_x:lines]
        when_start(*copies[4][:2])
        when_start(*copies[5][:2])
        rise_ref[...] = rise[0]
        fall_ref[...] = fall[0]
        x_send[step, 0] = rise_ref[pl.ds(0, brick_z, stride=brick_x), :]
        x_send[step, 1] = fall_ref[pl.ds(brick_x - 1, brick_z, stride=brick_x), :]
        when_start(*copies[0][:2])
        when_start(*copies[1][:2])
        edge = jnp.where(y_pos == 0, rise[1], jnp.where(y_pos == brick_y - 1, fall[1], 0.0))
        edge_high, edge_low = parts(edge)
        edge_rows = dot(take, edge_high, NT) + dot(take, edge_low, NT)
        y_send[step, 0] = edge_rows[0:ROWS]
        y_send[step, 1] = edge_rows[ROWS:2 * ROWS]
        when_start(*copies[2][:2])
        when_start(*copies[3][:2])

        rest = 1.0 - (courant_ref[0] + courant_ref[1] + courant_ref[2])
        updated = rest * adjoint
        updated = updated + jnp.where(
            x_pos == brick_x - 1, 0.0, pltpu.roll(rise[0], lines - 1, 0)
        )
        updated = updated + jnp.where(x_pos == 0, 0.0, pltpu.roll(fall[0], 1, 0))
        updated = updated + jnp.where(
            y_pos == brick_y - 1, 0.0, pltpu.roll(rise[1], brick_y - 1, 1)
        )
        updated = updated + jnp.where(y_pos == 0, 0.0, pltpu.roll(fall[1], 1, 1))
        border = jnp.zeros((brick_x, brick_y), jnp.float32)
        updated = updated + jnp.concatenate([rise[2][brick_x:], border], axis=0)
        updated = updated + jnp.concatenate([border, fall[2][:lines - brick_x]], axis=0)
        sum_ref[...] = updated

        for copy, _, gets in copies:
            @pl.when(gets)
            def _():
                copy.wait_recv()

        top = pl.ds(brick_x - 1, brick_z, stride=brick_x)
        bottom = pl.ds(0, brick_z, stride=brick_x)
        sum_ref[top, :] = sum_ref[top, :] + x_recv[step, 0]
        sum_ref[bottom, :] = sum_ref[bottom, :] + x_recv[step, 1]
        last = pl.ds(lines - brick_x, brick_x)
        sum_ref[last, :] = sum_ref[last, :] + z_recv[step, 0]
        first = pl.ds(0, brick_x)
        sum_ref[first, :] = sum_ref[first, :] + z_recv[step, 1]
        side_rows = jnp.concatenate([y_recv[step, 0], y_recv[step, 1]], axis=0)
        side_high, side_low = parts(side_rows)
        adjoint = sum_ref[...] + (dot(side_high, put, TN) + dot(side_low, put, TN))
        tracer_loads[step].wait()
        if step == steps - 1:
            gradient = adjoint * tracer_ref[step]
        else:
            gradient = grad_ref[...] + adjoint * tracer_ref[step]
        grad_ref[...] = gradient

    from_end = jnp.where(take_row < ROWS, brick_y - take_lane, take_lane + 1)
    pull = jnp.exp(from_end.astype(jnp.float32) * (-1.0 / length)) / math.sqrt(length)
    carries = dot_three(pull, gradient, NT)
    packed = [
        carries[row:row + 1, t * LANES:(t + 1) * LANES] for row in (0, ROWS) for t in range(tiles)
    ]
    carry_send[...] = jnp.concatenate(packed, axis=0)
    carry_copies = []
    for d in range(1, n_gy):
        for moved, back in ((b + d, b - d), (b - d, b + d)):
            copy = pltpu.make_async_remote_copy(
                src_ref=carry_send,
                dst_ref=carry_recv.at[b],
                send_sem=carry_send_sem.at[rem(moved + n_gy, n_gy)],
                recv_sem=carry_recv_sem.at[b],
                device_id=(a, rem(moved + n_gy, n_gy), c),
                device_id_type=MESH,
            )
            arrival = pltpu.make_async_remote_copy(
                src_ref=carry_send,
                dst_ref=carry_recv.at[rem(back + n_gy, n_gy)],
                send_sem=carry_send_sem.at[rem(back + n_gy, n_gy)],
                recv_sem=carry_recv_sem.at[rem(back + n_gy, n_gy)],
                device_id=(a, rem(moved + n_gy, n_gy), c),
                device_id_type=MESH,
            )
            sends = (moved >= 0) & (moved < n_gy)
            gets = (back >= 0) & (back < n_gy)
            when_start(copy, sends)
            carry_copies.append((copy, sends, arrival, gets))

    high, low = parts(gradient)
    bulk_send[...] = (
        dot(y_high[...], high, NT) + dot(y_low[...], high, NT) + dot(y_high[...], low, NT)
    )

    mine = a * n_gz + c

    def bulk_copy(d):
        share = rem(mine + d, shares)
        other = b * shares + share
        return other, pltpu.make_async_remote_copy(
            src_ref=bulk_send.at[pl.ds(pl.multiple_of(share * pad_rows, ROWS), pad_rows), :],
            dst_ref=bulk_recv.at[mine],
            send_sem=bulk_send_sem.at[share],
            recv_sem=bulk_recv_sem.at[mine],
            device_id=(
                div(other, n_gy * n_gz), rem(div(other, n_gz), n_gy), rem(other, n_gz)
            ),
            device_id_type=MESH,
        )

    def bulk_start(d):
        other, copy = bulk_copy(d)

        @pl.when(other != me)
        def _():
            copy.start()

    each(0, shares, bulk_start)
    lambda_ref[...] = adjoint
    lambda_copy = pltpu.make_async_copy(lambda_ref, lambda_any, lambda_sem)
    lambda_copy.start()

    own = div(me, shares) == b

    @pl.when(own)
    def _():
        rows = pl.ds(pl.multiple_of((me - b * shares) * pad_rows, ROWS), pad_rows)
        bulk_recv[mine] = bulk_send[rows, :]

    for _, _, arrival, gets in carry_copies:
        @pl.when(gets)
        def _():
            arrival.wait_recv()

    carry_row = iota((2 * tiles, LANES), 0)
    entering = jnp.zeros((2 * tiles, LANES), jnp.float32)
    for brick in range(n_gy):
        between = jnp.where(carry_row < tiles, b - brick - 1, brick - b - 1)
        weight = jnp.exp(jnp.maximum(between, 0).astype(jnp.float32) * (-brick_y / length))
        entering = entering + jnp.where(between >= 0, weight, 0.0) * carry_recv[brick]
    enter_send[...] = entering

    def enter_copy(d):
        share = rem(mine + d, shares)
        other = b * shares + share
        return other, pltpu.make_async_remote_copy(
            src_ref=enter_send,
            dst_ref=enter_recv.at[mine],
            send_sem=enter_send_sem.at[share],
            recv_sem=enter_recv_sem.at[mine],
            device_id=(
                div(other, n_gy * n_gz), rem(div(other, n_gz), n_gy), rem(other, n_gz)
            ),
            device_id_type=MESH,
        )

    def enter_start(d):
        other, copy = enter_copy(d)

        @pl.when(other != me)
        def _():
            copy.start()

    each(0, shares, enter_start)

    @pl.when(own)
    def _():
        enter_recv[mine] = enter_send[...]

    for copy, sends, _ in all_copies:
        @pl.when(sends)
        def _():
            copy.wait_send()

    for copy, sends, _, _ in carry_copies:
        @pl.when(sends)
        def _():
            copy.wait_send()

    at_y = rem(me, shares) * y_rows + iota((pad_rows, LANES), 0)
    from_low = jnp.exp(at_y.astype(jnp.float32) * (-1.0 / length))
    from_high = jnp.exp(jnp.maximum(brick_y - 1 - at_y, 0).astype(jnp.float32) * (-1.0 / length))
    for i in range(n_gx):
        for k in range(n_gz):
            slot = i * n_gz + k

            @pl.when(jnp.logical_not(own & (mine == slot)))
            def _():
                for send, recv, send_sem, recv_sem in (
                    (bulk_send.at[pl.ds(0, pad_rows), :], bulk_recv, bulk_send_sem, bulk_recv_sem),
                    (enter_send, enter_recv, enter_send_sem, enter_recv_sem),
                ):
                    pltpu.make_async_remote_copy(
                        src_ref=send,
                        dst_ref=recv.at[slot],
                        send_sem=send_sem.at[slot],
                        recv_sem=recv_sem.at[slot],
                        device_id=(a, b, c),
                        device_id_type=MESH,
                    ).wait_recv()

        rows = []
        for k in range(n_gz):
            slot = i * n_gz + k
            for t in range(tiles):
                rows.append(
                    bulk_recv[slot, :, t * LANES:(t + 1) * LANES]
                    + from_low * enter_recv[slot, t:t + 1, :]
                    + from_high * enter_recv[slot, tiles + t:tiles + t + 1, :]
                )
        high, low = parts(jnp.concatenate(rows, axis=0))
        block_high = table_high[i * LANES:(i + 1) * LANES, :]
        block_low = table_low[i * LANES:(i + 1) * LANES, :]
        product = dot(high, block_high, NN) + dot(low, block_high, NN) + dot(high, block_low, NN)
        wide_ref[...] = product if i == 0 else wide_ref[...] + product

    def bulk_sent(d):
        other, copy = bulk_copy(d)
        _, enter = enter_copy(d)

        @pl.when(other != me)
        def _():
            copy.wait_send()
            enter.wait_send()

    each(0, shares, bulk_sent)
    each(1, groups, well_sent)
    lambda_copy.wait()


def depth_kernel(
    sizes, lambda_ref, wide_ref, lambda_out, smooth_ref, stage_ref=None
):
    brick_z, full_z, full_x, y_rows, pad_rows, tile_z = sizes
    wide_x = round_up(full_x, LANES)
    lambda_out[...] = lambda_ref[...]

    fade = math.exp(-0.5 / brick_z)

    def plane(z):
        row, depth = z // tile_z * pad_rows, z % tile_z
        return wide_ref[row:row + y_rows, depth * wide_x:(depth + 1) * wide_x]

    ahead = [plane(0)]
    for z in range(1, full_z):
        ahead.append(plane(z) + fade * ahead[-1])
    behind = None
    for z in reversed(range(full_z)):
        total = ahead[z] if behind is None else ahead[z] + behind
        if full_x <= LANES:
            smooth_ref[pl.ds(z, y_rows, stride=full_z), :] = total[:, 0:full_x]
        else:
            for tile in range(wide_x // LANES):
                part = total[:, tile * LANES:(tile + 1) * LANES]
                stage_ref[tile, pl.ds(z, y_rows, stride=full_z), :] = part
        behind = fade * (plane(z) if behind is None else plane(z) + behind)

    if full_x > LANES:
        for tile in range(wide_x // LANES):
            end = min((tile + 1) * LANES, full_x)
            smooth_ref[:, tile * LANES:end] = stage_ref[tile][:, 0:end - tile * LANES]


def per_device(well_sources, well_owner, well_cell, flow_sign, courant, tracer):
    steps, brick_z, brick_x, brick_y = tracer.shape
    n_gx, n_gy, n_gz = lax.axis_size("gx"), lax.axis_size("gy"), lax.axis_size("gz")
    groups, shares = n_gx * n_gy, n_gx * n_gz
    wells = well_cell.shape[0]
    cap = round_up(-(-wells // groups), ROWS)
    lines = brick_z * brick_x
    y_rows = brick_y // shares
    pad_rows = round_up(y_rows, ROWS)
    full_x, full_z = n_gx * brick_x, n_gz * brick_z
    wide_x = round_up(full_x, LANES)
    tile_z = LANES // brick_x
    tiles = lines // LANES
    f32 = jnp.float32
    sizes = (n_gx, n_gy, n_gz, brick_z, brick_x, brick_y, cap)
    dma = pltpu.SemaphoreType.DMA
    vmem = pl.BlockSpec(memory_space=pltpu.VMEM)
    away = pl.BlockSpec(memory_space=pl.ANY)
    field = (3, lines, brick_y)
    stage = []
    if full_x > LANES:
        stage = [pltpu.VMEM((wide_x // LANES, y_rows * full_z, LANES), f32)]
    run = pl.pallas_call(
        functools.partial(kernel, sizes),
        out_shape=(
            jax.ShapeDtypeStruct((lines, brick_y), f32),
            jax.ShapeDtypeStruct((n_gz * tiles * pad_rows, tile_z * wide_x), f32),
        ),
        in_specs=[away] * 6,
        out_specs=(away, vmem),
        scratch_shapes=[
            pltpu.VMEM((lines, brick_y), f32),
            dma,
            pltpu.VMEM((brick_z, wells), f32),
            pltpu.VMEM((1, wells), jnp.int32),
            pltpu.VMEM((1, wells), jnp.int32),
            dma((3,)),
            pltpu.VMEM((steps, lines, brick_y), jnp.int32),
            pltpu.VMEM(field, f32),
            pltpu.VMEM((steps, lines, brick_y), f32),
            dma((2, steps + 1)),
            pltpu.VMEM((LANES, wells), f32),
            pltpu.VMEM((groups * cap, LANES), f32),
            pltpu.VMEM((groups * cap, LANES), f32),
            dma((groups,)),
            dma((groups,)),
            pltpu.VMEM((lines, brick_y), f32),
            pltpu.VMEM((lines, brick_y), f32),
            pltpu.VMEM((lines, brick_y), f32),
            pltpu.VMEM((lines, brick_y), f32),
            pltpu.VMEM((steps, 2, brick_z, brick_y), f32),
            pltpu.VMEM((steps, 2, brick_z, brick_y), f32),
            pltpu.VMEM((steps, 2, ROWS, lines), f32),
            pltpu.VMEM((steps, 2, ROWS, lines), f32),
            pltpu.VMEM((steps, 2, brick_x, brick_y), f32),
            pltpu.VMEM((steps, 2, brick_x, brick_y), f32),
            dma((steps, 3, 2)),
            dma((steps, 3, 2)),
            pltpu.VMEM((2 * tiles, LANES), f32),
            pltpu.VMEM((n_gy, 2 * tiles, LANES), f32),
            dma((n_gy,)),
            dma((n_gy,)),
            pltpu.VMEM((2 * tiles, LANES), f32),
            pltpu.VMEM((shares, 2 * tiles, LANES), f32),
            dma((shares,)),
            dma((shares,)),
            pltpu.VMEM((shares * pad_rows, lines), f32),
            pltpu.VMEM((shares, pad_rows, lines), f32),
            dma((shares,)),
            dma((shares,)),
            pltpu.VMEM((n_gx * LANES, tile_z * wide_x), jnp.bfloat16),
            pltpu.VMEM((n_gx * LANES, tile_z * wide_x), jnp.bfloat16),
            pltpu.VMEM((shares * pad_rows, brick_y), jnp.bfloat16),
            pltpu.VMEM((shares * pad_rows, brick_y), jnp.bfloat16),
        ],
        compiler_params=pltpu.CompilerParams(
            collective_id=0, has_side_effects=True, vmem_limit_bytes=56 * 2**20
        ),
    )
    start, wide = run(
        well_sources.T,
        well_owner.reshape(1, wells),
        well_cell.reshape(1, wells),
        flow_sign.reshape(steps, lines, brick_y),
        courant.reshape(field),
        tracer.reshape(steps, lines, brick_y),
    )
    depth_sizes = (brick_z, full_z, full_x, y_rows, pad_rows, tile_z)
    start, smoothed = pl.pallas_call(
        functools.partial(depth_kernel, depth_sizes),
        out_shape=(
            jax.ShapeDtypeStruct((lines, brick_y), f32),
            jax.ShapeDtypeStruct((y_rows * full_z, full_x), f32),
        ),
        in_specs=[vmem, vmem],
        out_specs=(vmem, vmem),
        scratch_shapes=stage,
    )(start, wide)
    return (
        start.reshape(brick_z, brick_x, brick_y),
        smoothed.reshape(y_rows, full_z, full_x),
    )


def solution(mesh):
    return jax.shard_map(
        per_device,
        mesh=mesh,
        in_specs=(
            P(("gx", "gy"), "gz"),
            P(("gx", "gy"), None),
            P(("gx", "gy")),
            P(None, "gz", "gx", "gy"),
            P(None, "gz", "gx", "gy"),
            P(None, "gz", "gx", "gy"),
        ),
        out_specs=(P("gz", "gx", "gy"), P(("gx", "gy", "gz"), None, None)),
        check_vma=False,
    )
```

```python
import functools
import math

import jax
import jax.numpy as jnp
from jax import lax
from jax.experimental import pallas as pl
from jax.experimental.pallas import tpu as pltpu
from jax.sharding import PartitionSpec as P

MESH = pl.DeviceIdType.MESH
LANES = 128
ROWS = 8


def round_up(value, unit):
    return -(-value // unit) * unit


def iota(shape, dim):
    return lax.broadcasted_iota(jnp.int32, shape, dim)


def div(value, by):
    return value >> (by.bit_length() - 1) if by & (by - 1) == 0 else lax.div(value, by)


def rem(value, by):
    return value & (by - 1) if by & (by - 1) == 0 else lax.rem(value, by)


def each(start, stop, act):
    if stop - start <= 32:
        for i in range(start, stop):
            act(i)
    else:
        lax.fori_loop(start, stop, lambda i, carried: (act(i), carried)[1], 0)


def parts(value):
    high = value.astype(jnp.bfloat16)
    return high, (value - high.astype(jnp.float32)).astype(jnp.bfloat16)


def dot(left, right, dims):
    return lax.dot_general(left, right, (dims, ((), ())), preferred_element_type=jnp.float32)


NN = ((1,), (0,))
NT = ((1,), (1,))
TN = ((0,), (0,))


def flag(mask):
    return jnp.where(mask, 1.0, 0.0).astype(jnp.bfloat16)


def dot_three(left, right, dims):
    left_high, left_low = parts(left)
    right_high, right_low = parts(right)
    return (
        dot(left_high, right_high, dims)
        + dot(left_low, right_high, dims)
        + dot(left_high, right_low, dims)
    )


def kernel(
    sizes, source_any, owner_any, cell_any, flow_any, courant_any, tracer_any,
    lambda_any, wide_ref, lambda_ref, lambda_sem,
    source_ref, owner_ref, cell_ref, small_sem,
    flow_ref, courant_ref, tracer_ref, load_sem,
    payload_ref, well_send, well_recv, well_send_sem, well_recv_sem,
    sum_ref, grad_ref,
    x_send, x_recv, y_send, y_recv, z_send, z_recv, face_send_sem, face_recv_sem,
    carry_send, carry_recv, carry_send_sem, carry_recv_sem,
    enter_send, enter_recv, enter_send_sem, enter_recv_sem,
    bulk_send, bulk_recv, bulk_send_sem, bulk_recv_sem,
    table_high, table_low, y_high, y_low,
):
    n_gx, n_gy, n_gz, brick_z, brick_x, brick_y, cap = sizes
    steps = flow_any.shape[0]
    length = 2.0 * brick_y
    lines = brick_z * brick_x
    groups = n_gx * n_gy
    devices = groups * n_gz
    a, b, c = lax.axis_index("gx"), lax.axis_index("gy"), lax.axis_index("gz")
    group = a * n_gy + b
    me = group * n_gz + c
    wells = source_any.shape[1]
    full_z = n_gz * brick_z
    full_x = n_gx * brick_x
    wide_x = round_up(full_x, LANES)
    shares = n_gx * n_gz
    y_rows = brick_y // shares
    pad_rows = round_up(y_rows, ROWS)
    tiles = lines // LANES
    tile_z = LANES // brick_x

    for ref in (x_recv, y_recv, z_recv, carry_recv):
        ref[...] = jnp.zeros_like(ref)

    barrier = pltpu.get_barrier_semaphore()

    def greet(d):
        other = rem(me + d, devices)
        pl.semaphore_signal(
            barrier, inc=1,
            device_id=(
                div(other, n_gy * n_gz), rem(div(other, n_gz), n_gy), rem(other, n_gz)
            ),
            device_id_type=MESH,
        )

    each(1, devices, greet)
    small_loads = [
        pltpu.make_async_copy(src, dst, small_sem.at[i])
        for i, (src, dst) in enumerate(
            ((owner_any, owner_ref), (cell_any, cell_ref), (source_any, source_ref))
        )
    ]
    for load in small_loads:
        load.start()
    courant_load = pltpu.make_async_copy(courant_any, courant_ref, load_sem.at[0, steps])
    courant_load.start()
    flow_loads, tracer_loads = (
        [
            pltpu.make_async_copy(src.at[step], dst.at[step], load_sem.at[kind, step])
            for step in range(steps)
        ]
        for kind, (src, dst) in enumerate(((flow_any, flow_ref), (tracer_any, tracer_ref)))
    )
    for step in reversed(range(steps)):
        flow_loads[step].start()
        tracer_loads[step].start()

    eye = iota((wells, wells), 0) == iota((wells, wells), 1)
    before = iota((wells, wells), 0) < iota((wells, wells), 1)
    for load in small_loads:
        load.wait()
    owner_row = owner_ref[...].astype(jnp.float32)
    owner_col = jnp.sum(jnp.where(eye, owner_row, 0.0), axis=1, keepdims=True)
    rank_row = jnp.sum(
        jnp.where(before & (owner_col == owner_row), 1.0, 0.0), axis=0, keepdims=True
    )
    slots = groups * cap
    second = rank_row >= cap
    key_row = owner_row * cap + rank_row + jnp.where(second, slots - cap, 0)
    chosen = flag(iota((2 * slots, wells), 0) == key_row.astype(jnp.int32))
    cell_row = cell_ref[...]
    payload_ref[...] = jnp.zeros_like(payload_ref)
    payload_ref[0:brick_z, :] = source_ref[...]
    payload_ref[brick_z:brick_z + 1, :] = div(cell_row, brick_y).astype(jnp.float32)
    payload_ref[brick_z + 1:brick_z + 2, :] = rem(cell_row, brick_y).astype(jnp.float32)
    payload_high, payload_low = parts(payload_ref[...])
    sorted_wells = dot(chosen, payload_high, NT) + dot(chosen, payload_low, NT)
    well_send[...] = sorted_wells[0:slots] + pltpu.roll(sorted_wells[slots:], LANES // 2, 1)

    pl.semaphore_wait(barrier, devices - 1)

    def group_rows(index):
        return pl.ds(pl.multiple_of(index * cap, ROWS), cap)

    def well_copy(d):
        other = rem(group + d, groups)
        return pltpu.make_async_remote_copy(
            src_ref=well_send.at[group_rows(other), :],
            dst_ref=well_recv.at[group_rows(group), :],
            send_sem=well_send_sem.at[d],
            recv_sem=well_recv_sem.at[d],
            device_id=(div(other, n_gy), rem(other, n_gy), c),
            device_id_type=MESH,
        )

    def well_start(d):
        well_copy(d).start()

    each(1, groups, well_start)
    well_recv[group_rows(group), :] = well_send[group_rows(group), :]

    shape = (n_gx * LANES, wide_x)
    at_x = div(iota(shape, 0), LANES) * brick_x + rem(iota(shape, 0), brick_x)
    far = jnp.abs(at_x - iota(shape, 1)).astype(jnp.float32)
    table = jnp.exp(far * (-0.5 / brick_x)) / math.sqrt(2 * brick_x) / math.sqrt(2 * brick_z)
    table = jnp.where(iota(shape, 1) < full_x, table, 0.0)
    depth_of = rem(div(iota(shape, 0), brick_x), tile_z)
    for depth in range(tile_z):
        high, low = parts(jnp.where(depth_of == depth, table, 0.0))
        table_high[:, depth * wide_x:(depth + 1) * wide_x] = high
        table_low[:, depth * wide_x:(depth + 1) * wide_x] = low

    def line_place(row):
        return div(row, pad_rows) * y_rows + rem(row, pad_rows)

    shape = (shares * pad_rows, brick_y)
    near = jnp.abs(line_place(iota(shape, 0)) - iota(shape, 1)).astype(jnp.float32)
    table_y = jnp.exp(near * (-1.0 / length)) / math.sqrt(length)
    take_row, take_lane = iota((2 * ROWS, brick_y), 0), iota((2 * ROWS, brick_y), 1)
    from_end = jnp.where(take_row < ROWS, brick_y - take_lane, take_lane + 1)
    pull = jnp.exp(from_end.astype(jnp.float32) * (-1.0 / length)) / math.sqrt(length)
    y_high[...], y_low[...] = parts(jnp.concatenate([table_y, pull], axis=0))

    spread = flag(div(iota((lines, LANES), 0), brick_x) == iota((lines, LANES), 1))
    x_pick = flag(iota((ROWS, LANES), 1) == brick_z)

    courant_load.wait()

    def well_wait(d):
        well_copy(d).wait_recv()

    def well_sent(d):
        well_copy(d).wait_send()

    each(1, groups, well_wait)
    landed = well_recv[...]
    landed = jnp.concatenate([landed, pltpu.roll(landed, LANES // 2, 1)], axis=0)
    landed_high, landed_low = parts(landed)
    x_row = dot(x_pick, landed_high, NT)[0:1, :].astype(jnp.int32)
    x_hit = rem(iota((lines, 2 * slots), 0), brick_x) == x_row
    y_hit = flag(
        iota((2 * slots, LANES), 1) == landed[:, brick_z + 1:brick_z + 2].astype(jnp.int32)
    )
    spread_high = jnp.where(x_hit, dot(spread, landed_high, NT), 0.0).astype(jnp.bfloat16)
    spread_low = jnp.where(x_hit, dot(spread, landed_low, NT), 0.0).astype(jnp.bfloat16)
    adjoint = dot(spread_high, y_hit, NN) + dot(spread_low, y_hit, NN)

    y_pos = iota((lines, brick_y), 1)
    x_pos = rem(iota((lines, brick_y), 0), brick_x)
    take = flag(
        ((take_row < ROWS) & (take_lane == 0)) | ((take_row >= ROWS) & (take_lane == brick_y - 1))
    )
    put = flag(
        ((take_row == 0) & (take_lane == brick_y - 1)) | ((take_row == ROWS) & (take_lane == 0))
    )

    def face_copies(step):
        copies = []
        for axis, (place, count, send, recv) in enumerate(
            ((a, n_gx, x_send, x_recv), (b, n_gy, y_send, y_recv), (c, n_gz, z_send, z_recv))
        ):
            for side in range(2):
                moved = place - 1 if side == 0 else place + 1
                target = [a, b, c]
                target[axis] = rem(moved + count, count)
                sends = place > 0 if side == 0 else place < count - 1
                gets = place < count - 1 if side == 0 else place > 0
                copy = pltpu.make_async_remote_copy(
                    src_ref=send.at[step, side],
                    dst_ref=recv.at[step, side],
                    send_sem=face_send_sem.at[step, axis, side],
                    recv_sem=face_recv_sem.at[step, axis, side],
                    device_id=tuple(target),
                    device_id_type=MESH,
                )
                copies.append((copy, sends, gets))
        return copies

    def when_start(copy, sends):
        @pl.when(sends)
        def _():
            copy.start()

    all_copies = []
    for step in reversed(range(steps)):
        copies = face_copies(step)
        all_copies.extend(copies)
        flow_loads[step].wait()
        sum_ref[...] = adjoint
        last_x = pl.ds(brick_x - 1, brick_z, stride=brick_x)
        first_x = pl.ds(0, brick_z, stride=brick_x)
        last_z, first_z = pl.ds(lines - brick_x, brick_x), pl.ds(0, brick_x)
        flow = flow_ref[step]
        flow_y = courant_ref[1] * adjoint
        rise_y = jnp.where((flow & 2) != 0, flow_y, 0.0)
        fall_y = flow_y - rise_y
        edge = jnp.where(y_pos == 0, rise_y, jnp.where(y_pos == brick_y - 1, fall_y, 0.0))
        edge_high, edge_low = parts(edge)
        edge_rows = dot(take, edge_high, NT) + dot(take, edge_low, NT)
        for axis, send, ends in ((0, x_send, (first_x, last_x)), (2, z_send, (first_z, last_z))):
            for side, rows in enumerate(ends):
                up = (flow_ref[step, rows, :] & (1 << axis)) != 0
                leaving = up if side == 0 else jnp.logical_not(up)
                send[step, side] = jnp.where(
                    leaving, courant_ref[axis, rows, :] * sum_ref[rows, :], 0.0
                )
        y_send[step, 0] = edge_rows[0:ROWS]
        y_send[step, 1] = edge_rows[ROWS:2 * ROWS]
        for copy, sends, _ in copies:
            when_start(copy, sends)

        flow_x, flow_z = courant_ref[0] * adjoint, courant_ref[2] * adjoint
        rise_x = jnp.where((flow & 1) != 0, flow_x, 0.0)
        rise_z = jnp.where((flow & 4) != 0, flow_z, 0.0)
        rise = [rise_x, rise_y, rise_z]
        fall = [flow_x - rise_x, fall_y, flow_z - rise_z]
        rest = 1.0 - (courant_ref[0] + courant_ref[1] + courant_ref[2])
        updated = rest * adjoint
        updated = updated + jnp.where(
            x_pos == brick_x - 1, 0.0, pltpu.roll(rise[0], lines - 1, 0)
        )
        updated = updated + jnp.where(x_pos == 0, 0.0, pltpu.roll(fall[0], 1, 0))
        updated = updated + jnp.where(
            y_pos == brick_y - 1, 0.0, pltpu.roll(rise[1], brick_y - 1, 1)
        )
        updated = updated + jnp.where(y_pos == 0, 0.0, pltpu.roll(fall[1], 1, 1))
        border = jnp.zeros((brick_x, brick_y), jnp.float32)
        updated = updated + jnp.concatenate([rise[2][brick_x:], border], axis=0)
        updated = updated + jnp.concatenate([border, fall[2][:lines - brick_x]], axis=0)
        sum_ref[...] = updated

        for copy, _, gets in copies:
            @pl.when(gets)
            def _():
                copy.wait_recv()

        for rows, recv, side in (
            (last_x, x_recv, 0), (first_x, x_recv, 1), (last_z, z_recv, 0), (first_z, z_recv, 1)
        ):
            sum_ref[rows, :] = sum_ref[rows, :] + recv[step, side]
        side_rows = jnp.concatenate([y_recv[step, 0], y_recv[step, 1]], axis=0)
        side_high, side_low = parts(side_rows)
        adjoint = sum_ref[...] + (dot(side_high, put, TN) + dot(side_low, put, TN))
        tracer_loads[step].wait()
        if step == steps - 1:
            gradient = adjoint * tracer_ref[step]
        else:
            gradient = grad_ref[...] + adjoint * tracer_ref[step]
        grad_ref[...] = gradient

    high, low = parts(gradient)
    smooth_y = (
        dot(y_high[...], high, NT) + dot(y_low[...], high, NT) + dot(y_high[...], low, NT)
    )
    bulk_send[...] = smooth_y[0:shares * pad_rows]
    carries = smooth_y[shares * pad_rows:]
    packed = [
        carries[row:row + 1, t * LANES:(t + 1) * LANES] for row in (0, ROWS) for t in range(tiles)
    ]
    carry_send[...] = jnp.concatenate(packed, axis=0)
    carry_copies = []
    for d in range(1, n_gy):
        for moved, back in ((b + d, b - d), (b - d, b + d)):
            copy = pltpu.make_async_remote_copy(
                src_ref=carry_send,
                dst_ref=carry_recv.at[b],
                send_sem=carry_send_sem.at[rem(moved + n_gy, n_gy)],
                recv_sem=carry_recv_sem.at[b],
                device_id=(a, rem(moved + n_gy, n_gy), c),
                device_id_type=MESH,
            )
            arrival = pltpu.make_async_remote_copy(
                src_ref=carry_send,
                dst_ref=carry_recv.at[rem(back + n_gy, n_gy)],
                send_sem=carry_send_sem.at[rem(back + n_gy, n_gy)],
                recv_sem=carry_recv_sem.at[rem(back + n_gy, n_gy)],
                device_id=(a, rem(moved + n_gy, n_gy), c),
                device_id_type=MESH,
            )
            sends = (moved >= 0) & (moved < n_gy)
            gets = (back >= 0) & (back < n_gy)
            when_start(copy, sends)
            carry_copies.append((copy, sends, arrival, gets))

    mine = a * n_gz + c

    def far_first(d):
        return jnp.where(2 * b < n_gy, shares - 1 - d, d)

    def bulk_copy(d):
        share = far_first(d)
        other = b * shares + share
        return other, pltpu.make_async_remote_copy(
            src_ref=bulk_send.at[pl.ds(pl.multiple_of(share * pad_rows, ROWS), pad_rows), :],
            dst_ref=bulk_recv.at[mine],
            send_sem=bulk_send_sem.at[share],
            recv_sem=bulk_recv_sem.at[mine],
            device_id=(
                div(other, n_gy * n_gz), rem(div(other, n_gz), n_gy), rem(other, n_gz)
            ),
            device_id_type=MESH,
        )

    def bulk_start(d):
        other, copy = bulk_copy(d)

        @pl.when(other != me)
        def _():
            copy.start()

    each(0, shares, bulk_start)
    lambda_ref[...] = adjoint
    lambda_copy = pltpu.make_async_copy(lambda_ref, lambda_any, lambda_sem)
    lambda_copy.start()

    own = div(me, shares) == b

    @pl.when(own)
    def _():
        rows = pl.ds(pl.multiple_of((me - b * shares) * pad_rows, ROWS), pad_rows)
        bulk_recv[mine] = bulk_send[rows, :]

    for _, _, arrival, gets in carry_copies:
        @pl.when(gets)
        def _():
            arrival.wait_recv()

    carry_row = iota((2 * tiles, LANES), 0)
    entering = jnp.zeros((2 * tiles, LANES), jnp.float32)
    for brick in range(n_gy):
        between = jnp.where(carry_row < tiles, b - brick - 1, brick - b - 1)
        weight = jnp.exp(jnp.maximum(between, 0).astype(jnp.float32) * (-brick_y / length))
        entering = entering + jnp.where(between >= 0, weight, 0.0) * carry_recv[brick]
    enter_send[...] = entering

    def enter_copy(d):
        share = far_first(d)
        other = b * shares + share
        return other, pltpu.make_async_remote_copy(
            src_ref=enter_send,
            dst_ref=enter_recv.at[mine],
            send_sem=enter_send_sem.at[share],
            recv_sem=enter_recv_sem.at[mine],
            device_id=(
                div(other, n_gy * n_gz), rem(div(other, n_gz), n_gy), rem(other, n_gz)
            ),
            device_id_type=MESH,
        )

    def enter_start(d):
        other, copy = enter_copy(d)

        @pl.when(other != me)
        def _():
            copy.start()

    each(0, shares, enter_start)

    @pl.when(own)
    def _():
        enter_recv[mine] = enter_send[...]

    for copy, sends, _ in all_copies:
        @pl.when(sends)
        def _():
            copy.wait_send()

    for copy, sends, _, _ in carry_copies:
        @pl.when(sends)
        def _():
            copy.wait_send()

    at_y = rem(me, shares) * y_rows + iota((pad_rows, LANES), 0)
    from_low = jnp.exp(at_y.astype(jnp.float32) * (-1.0 / length))
    from_high = jnp.exp(jnp.maximum(brick_y - 1 - at_y, 0).astype(jnp.float32) * (-1.0 / length))
    for i in range(n_gx):
        for k in range(n_gz):
            slot = i * n_gz + k

            @pl.when(jnp.logical_not(own & (mine == slot)))
            def _():
                for send, recv, send_sem, recv_sem in (
                    (bulk_send.at[pl.ds(0, pad_rows), :], bulk_recv, bulk_send_sem, bulk_recv_sem),
                    (enter_send, enter_recv, enter_send_sem, enter_recv_sem),
                ):
                    pltpu.make_async_remote_copy(
                        src_ref=send,
                        dst_ref=recv.at[slot],
                        send_sem=send_sem.at[slot],
                        recv_sem=recv_sem.at[slot],
                        device_id=(a, b, c),
                        device_id_type=MESH,
                    ).wait_recv()

        rows = []
        for k in range(n_gz):
            slot = i * n_gz + k
            for t in range(tiles):
                rows.append(
                    bulk_recv[slot, :, t * LANES:(t + 1) * LANES]
                    + from_low * enter_recv[slot, t:t + 1, :]
                    + from_high * enter_recv[slot, tiles + t:tiles + t + 1, :]
                )
        high, low = parts(jnp.concatenate(rows, axis=0))
        block_high = table_high[i * LANES:(i + 1) * LANES, :]
        block_low = table_low[i * LANES:(i + 1) * LANES, :]
        product = dot(high, block_high, NN) + dot(low, block_high, NN) + dot(high, block_low, NN)
        wide_ref[...] = product if i == 0 else wide_ref[...] + product

    def bulk_sent(d):
        other, copy = bulk_copy(d)
        _, enter = enter_copy(d)

        @pl.when(other != me)
        def _():
            copy.wait_send()
            enter.wait_send()

    each(0, shares, bulk_sent)
    each(1, groups, well_sent)
    lambda_copy.wait()


def depth_kernel(
    sizes, lambda_ref, wide_ref, lambda_out, smooth_ref, stage_ref=None
):
    brick_z, full_z, full_x, y_rows, pad_rows, tile_z = sizes
    wide_x = round_up(full_x, LANES)
    lambda_out[...] = lambda_ref[...]

    fade = math.exp(-0.5 / brick_z)

    def plane(z):
        row, depth = z // tile_z * pad_rows, z % tile_z
        return wide_ref[row:row + y_rows, depth * wide_x:(depth + 1) * wide_x]

    ahead = [plane(0)]
    for z in range(1, full_z):
        ahead.append(plane(z) + fade * ahead[-1])
    behind = None
    for z in reversed(range(full_z)):
        total = ahead[z] if behind is None else ahead[z] + behind
        if full_x <= LANES:
            smooth_ref[pl.ds(z, y_rows, stride=full_z), :] = total[:, 0:full_x]
        else:
            for tile in range(wide_x // LANES):
                part = total[:, tile * LANES:(tile + 1) * LANES]
                stage_ref[tile, pl.ds(z, y_rows, stride=full_z), :] = part
        behind = fade * (plane(z) if behind is None else plane(z) + behind)

    if full_x > LANES:
        for tile in range(wide_x // LANES):
            end = min((tile + 1) * LANES, full_x)
            smooth_ref[:, tile * LANES:end] = stage_ref[tile][:, 0:end - tile * LANES]


def per_device(well_sources, well_owner, well_cell, flow_sign, courant, tracer):
    steps, brick_z, brick_x, brick_y = tracer.shape
    n_gx, n_gy, n_gz = lax.axis_size("gx"), lax.axis_size("gy"), lax.axis_size("gz")
    groups, shares = n_gx * n_gy, n_gx * n_gz
    wells = well_cell.shape[0]
    cap = round_up(-(-wells // groups), ROWS)
    lines = brick_z * brick_x
    y_rows = brick_y // shares
    pad_rows = round_up(y_rows, ROWS)
    full_x, full_z = n_gx * brick_x, n_gz * brick_z
    wide_x = round_up(full_x, LANES)
    tile_z = LANES // brick_x
    tiles = lines // LANES
    f32 = jnp.float32
    sizes = (n_gx, n_gy, n_gz, brick_z, brick_x, brick_y, cap)
    dma = pltpu.SemaphoreType.DMA
    vmem = pl.BlockSpec(memory_space=pltpu.VMEM)
    away = pl.BlockSpec(memory_space=pl.ANY)
    field = (3, lines, brick_y)
    stage = []
    if full_x > LANES:
        stage = [pltpu.VMEM((wide_x // LANES, y_rows * full_z, LANES), f32)]
    run = pl.pallas_call(
        functools.partial(kernel, sizes),
        out_shape=(
            jax.ShapeDtypeStruct((lines, brick_y), f32),
            jax.ShapeDtypeStruct((n_gz * tiles * pad_rows, tile_z * wide_x), f32),
        ),
        in_specs=[away] * 6,
        out_specs=(away, vmem),
        scratch_shapes=[
            pltpu.VMEM((lines, brick_y), f32),
            dma,
            pltpu.VMEM((brick_z, wells), f32),
            pltpu.VMEM((1, wells), jnp.int32),
            pltpu.VMEM((1, wells), jnp.int32),
            dma((3,)),
            pltpu.VMEM((steps, lines, brick_y), jnp.int32),
            pltpu.VMEM(field, f32),
            pltpu.VMEM((steps, lines, brick_y), f32),
            dma((2, steps + 1)),
            pltpu.VMEM((LANES, wells), f32),
            pltpu.VMEM((groups * cap, LANES), f32),
            pltpu.VMEM((groups * cap, LANES), f32),
            dma((groups,)),
            dma((groups,)),
            pltpu.VMEM((lines, brick_y), f32),
            pltpu.VMEM((lines, brick_y), f32),
            pltpu.VMEM((steps, 2, brick_z, brick_y), f32),
            pltpu.VMEM((steps, 2, brick_z, brick_y), f32),
            pltpu.VMEM((steps, 2, ROWS, lines), f32),
            pltpu.VMEM((steps, 2, ROWS, lines), f32),
            pltpu.VMEM((steps, 2, brick_x, brick_y), f32),
            pltpu.VMEM((steps, 2, brick_x, brick_y), f32),
            dma((steps, 3, 2)),
            dma((steps, 3, 2)),
            pltpu.VMEM((2 * tiles, LANES), f32),
            pltpu.VMEM((n_gy, 2 * tiles, LANES), f32),
            dma((n_gy,)),
            dma((n_gy,)),
            pltpu.VMEM((2 * tiles, LANES), f32),
            pltpu.VMEM((shares, 2 * tiles, LANES), f32),
            dma((shares,)),
            dma((shares,)),
            pltpu.VMEM((shares * pad_rows, lines), f32),
            pltpu.VMEM((shares, pad_rows, lines), f32),
            dma((shares,)),
            dma((shares,)),
            pltpu.VMEM((n_gx * LANES, tile_z * wide_x), jnp.bfloat16),
            pltpu.VMEM((n_gx * LANES, tile_z * wide_x), jnp.bfloat16),
            pltpu.VMEM((shares * pad_rows + 2 * ROWS, brick_y), jnp.bfloat16),
            pltpu.VMEM((shares * pad_rows + 2 * ROWS, brick_y), jnp.bfloat16),
        ],
        compiler_params=pltpu.CompilerParams(
            collective_id=0, has_side_effects=True, vmem_limit_bytes=56 * 2**20
        ),
    )
    start, wide = run(
        well_sources.T,
        well_owner.reshape(1, wells),
        well_cell.reshape(1, wells),
        flow_sign.reshape(steps, lines, brick_y),
        courant.reshape(field),
        tracer.reshape(steps, lines, brick_y),
    )
    depth_sizes = (brick_z, full_z, full_x, y_rows, pad_rows, tile_z)
    start, smoothed = pl.pallas_call(
        functools.partial(depth_kernel, depth_sizes),
        out_shape=(
            jax.ShapeDtypeStruct((lines, brick_y), f32),
            jax.ShapeDtypeStruct((y_rows * full_z, full_x), f32),
        ),
        in_specs=[vmem, vmem],
        out_specs=(vmem, vmem),
        scratch_shapes=stage,
    )(start, wide)
    return (
        start.reshape(brick_z, brick_x, brick_y),
        smoothed.reshape(y_rows, full_z, full_x),
    )


def solution(mesh):
    return jax.shard_map(
        per_device,
        mesh=mesh,
        in_specs=(
            P(("gx", "gy"), "gz"),
            P(("gx", "gy"), None),
            P(("gx", "gy")),
            P(None, "gz", "gx", "gy"),
            P(None, "gz", "gx", "gy"),
            P(None, "gz", "gx", "gy"),
        ),
        out_specs=(P("gz", "gx", "gy"), P(("gx", "gy", "gz"), None, None)),
        check_vma=False,
    )
```

```python
import functools
import math

import jax
import jax.numpy as jnp
from jax import lax
from jax.experimental import pallas as pl
from jax.experimental.pallas import tpu as pltpu
from jax.sharding import PartitionSpec as P

MESH = pl.DeviceIdType.MESH
LANES = 128
ROWS = 8


def round_up(value, unit):
    return -(-value // unit) * unit


def iota(shape, dim):
    return lax.broadcasted_iota(jnp.int32, shape, dim)


def div(value, by):
    return value >> (by.bit_length() - 1) if by & (by - 1) == 0 else lax.div(value, by)


def rem(value, by):
    return value & (by - 1) if by & (by - 1) == 0 else lax.rem(value, by)


def each(start, stop, act):
    if stop - start <= 32:
        for i in range(start, stop):
            act(i)
    else:
        lax.fori_loop(start, stop, lambda i, carried: (act(i), carried)[1], 0)


def parts(value):
    high = value.astype(jnp.bfloat16)
    return high, (value - high.astype(jnp.float32)).astype(jnp.bfloat16)


def lane_width(extent):
    return extent if LANES % extent == 0 else round_up(extent, LANES)


def dot(left, right, dims):
    return lax.dot_general(left, right, (dims, ((), ())), preferred_element_type=jnp.float32)


NN = ((1,), (0,))
NT = ((1,), (1,))
TN = ((0,), (0,))


def flag(mask):
    return jnp.where(mask, 1.0, 0.0).astype(jnp.bfloat16)


def dot_three(left, right, dims):
    left_high, left_low = parts(left)
    right_high, right_low = parts(right)
    return (
        dot(left_high, right_high, dims)
        + dot(left_low, right_high, dims)
        + dot(left_high, right_low, dims)
    )


def kernel(
    sizes, source_any, owner_any, cell_any, flow_any, courant_any, tracer_any,
    lambda_any, wide_ref, lambda_ref, lambda_sem,
    source_ref, owner_ref, cell_ref, small_sem,
    flow_ref, courant_ref, tracer_ref, load_sem,
    payload_ref, well_send, well_recv, well_send_sem, well_recv_sem,
    sum_ref, grad_ref,
    x_send, x_recv, y_send, y_recv, z_send, z_recv, face_send_sem, face_recv_sem,
    carry_send, carry_recv, carry_send_sem, carry_recv_sem,
    enter_send, enter_recv, enter_send_sem, enter_recv_sem,
    bulk_send, bulk_recv, bulk_send_sem, bulk_recv_sem,
    table_high, table_low, y_high, y_low,
):
    n_gx, n_gy, n_gz, brick_z, brick_x, brick_y, cap = sizes
    steps = flow_any.shape[0]
    length = 2.0 * brick_y
    lines = brick_z * brick_x
    groups = n_gx * n_gy
    devices = groups * n_gz
    a, b, c = lax.axis_index("gx"), lax.axis_index("gy"), lax.axis_index("gz")
    group = a * n_gy + b
    me = group * n_gz + c
    wells = source_any.shape[1]
    full_z = n_gz * brick_z
    full_x = n_gx * brick_x
    wide_x = lane_width(full_x)
    shares = n_gx * n_gz
    y_rows = brick_y // shares
    pad_rows = round_up(y_rows, ROWS)
    tiles = lines // LANES
    tile_z = LANES // brick_x

    for ref in (x_recv, y_recv, z_recv, carry_recv):
        ref[...] = jnp.zeros_like(ref)

    barrier = pltpu.get_barrier_semaphore()

    def greet(d):
        other = rem(me + d, devices)
        pl.semaphore_signal(
            barrier, inc=1,
            device_id=(
                div(other, n_gy * n_gz), rem(div(other, n_gz), n_gy), rem(other, n_gz)
            ),
            device_id_type=MESH,
        )

    each(1, devices, greet)
    small_loads = [
        pltpu.make_async_copy(src, dst, small_sem.at[i])
        for i, (src, dst) in enumerate(
            ((owner_any, owner_ref), (cell_any, cell_ref), (source_any, source_ref))
        )
    ]
    for load in small_loads:
        load.start()
    courant_load = pltpu.make_async_copy(courant_any, courant_ref, load_sem.at[0, steps])
    courant_load.start()
    flow_loads, tracer_loads = (
        [
            pltpu.make_async_copy(src.at[step], dst.at[step], load_sem.at[kind, step])
            for step in range(steps)
        ]
        for kind, (src, dst) in enumerate(((flow_any, flow_ref), (tracer_any, tracer_ref)))
    )
    for step in reversed(range(steps)):
        flow_loads[step].start()
        tracer_loads[step].start()

    eye = iota((wells, wells), 0) == iota((wells, wells), 1)
    before = iota((wells, wells), 0) < iota((wells, wells), 1)
    for load in small_loads:
        load.wait()
    owner_row = owner_ref[...].astype(jnp.float32)
    owner_col = jnp.sum(jnp.where(eye, owner_row, 0.0), axis=1, keepdims=True)
    rank_row = jnp.sum(
        jnp.where(before & (owner_col == owner_row), 1.0, 0.0), axis=0, keepdims=True
    )
    slots = groups * cap
    second = rank_row >= cap
    key_row = owner_row * cap + rank_row + jnp.where(second, slots - cap, 0)
    chosen = flag(iota((2 * slots, wells), 0) == key_row.astype(jnp.int32))
    cell_row = cell_ref[...]
    payload_ref[...] = jnp.zeros_like(payload_ref)
    payload_ref[0:brick_z, :] = source_ref[...]
    payload_ref[brick_z:brick_z + 1, :] = div(cell_row, brick_y).astype(jnp.float32)
    payload_ref[brick_z + 1:brick_z + 2, :] = rem(cell_row, brick_y).astype(jnp.float32)
    payload_high, payload_low = parts(payload_ref[...])
    sorted_wells = dot(chosen, payload_high, NT) + dot(chosen, payload_low, NT)
    well_send[...] = sorted_wells[0:slots] + pltpu.roll(sorted_wells[slots:], LANES // 2, 1)

    pl.semaphore_wait(barrier, devices - 1)

    def group_rows(index):
        return pl.ds(pl.multiple_of(index * cap, ROWS), cap)

    def well_copy(d):
        other = rem(group + d, groups)
        return pltpu.make_async_remote_copy(
            src_ref=well_send.at[group_rows(other), :],
            dst_ref=well_recv.at[group_rows(group), :],
            send_sem=well_send_sem.at[d],
            recv_sem=well_recv_sem.at[d],
            device_id=(div(other, n_gy), rem(other, n_gy), c),
            device_id_type=MESH,
        )

    def well_start(d):
        well_copy(d).start()

    each(1, groups, well_start)
    well_recv[group_rows(group), :] = well_send[group_rows(group), :]

    block = max(wide_x, LANES)
    shape = (n_gx * LANES, block)
    at_x = div(iota(shape, 0), LANES) * brick_x + rem(iota(shape, 0), brick_x)
    to_x = rem(iota(shape, 1), wide_x) if wide_x < LANES else iota(shape, 1)
    far = jnp.abs(at_x - to_x).astype(jnp.float32)
    table = jnp.exp(far * (-0.5 / brick_x)) / math.sqrt(2 * brick_x) / math.sqrt(2 * brick_z)
    table = jnp.where(to_x < full_x, table, 0.0)
    depth_of = rem(div(iota(shape, 0), brick_x), tile_z)
    if wide_x < LANES:
        depth_of = depth_of - div(iota(shape, 1), wide_x)
    for start in range(0, tile_z * wide_x, block):
        high, low = parts(jnp.where(depth_of == start // wide_x, table, 0.0))
        table_high[:, start:start + block] = high
        table_low[:, start:start + block] = low

    def line_place(row):
        return div(row, pad_rows) * y_rows + rem(row, pad_rows)

    shape = (shares * pad_rows, brick_y)
    near = jnp.abs(line_place(iota(shape, 0)) - iota(shape, 1)).astype(jnp.float32)
    table_y = jnp.exp(near * (-1.0 / length)) / math.sqrt(length)
    take_row, take_lane = iota((2 * ROWS, brick_y), 0), iota((2 * ROWS, brick_y), 1)
    from_end = jnp.where(take_row < ROWS, brick_y - take_lane, take_lane + 1)
    pull = jnp.exp(from_end.astype(jnp.float32) * (-1.0 / length)) / math.sqrt(length)
    y_high[...], y_low[...] = parts(jnp.concatenate([table_y, pull], axis=0))

    spread = flag(div(iota((lines, LANES), 0), brick_x) == iota((lines, LANES), 1))
    x_pick = flag(iota((ROWS, LANES), 1) == brick_z)

    courant_load.wait()

    def well_wait(d):
        well_copy(d).wait_recv()

    def well_sent(d):
        well_copy(d).wait_send()

    each(1, groups, well_wait)
    landed = well_recv[...]
    landed = jnp.concatenate([landed, pltpu.roll(landed, LANES // 2, 1)], axis=0)
    landed_high, landed_low = parts(landed)
    x_row = dot(x_pick, landed_high, NT)[0:1, :].astype(jnp.int32)
    x_hit = rem(iota((lines, 2 * slots), 0), brick_x) == x_row
    y_hit = flag(
        iota((2 * slots, LANES), 1) == landed[:, brick_z + 1:brick_z + 2].astype(jnp.int32)
    )
    spread_high = jnp.where(x_hit, dot(spread, landed_high, NT), 0.0).astype(jnp.bfloat16)
    spread_low = jnp.where(x_hit, dot(spread, landed_low, NT), 0.0).astype(jnp.bfloat16)
    adjoint = dot(spread_high, y_hit, NN) + dot(spread_low, y_hit, NN)

    y_pos = iota((lines, brick_y), 1)
    x_pos = rem(iota((lines, brick_y), 0), brick_x)
    take = flag(
        ((take_row < ROWS) & (take_lane == 0)) | ((take_row >= ROWS) & (take_lane == brick_y - 1))
    )
    put = flag(
        ((take_row == 0) & (take_lane == brick_y - 1)) | ((take_row == ROWS) & (take_lane == 0))
    )

    def face_copies(step):
        copies = []
        for axis, (place, count, send, recv) in enumerate(
            ((a, n_gx, x_send, x_recv), (b, n_gy, y_send, y_recv), (c, n_gz, z_send, z_recv))
        ):
            for side in range(2):
                moved = place - 1 if side == 0 else place + 1
                target = [a, b, c]
                target[axis] = rem(moved + count, count)
                sends = place > 0 if side == 0 else place < count - 1
                gets = place < count - 1 if side == 0 else place > 0
                copy = pltpu.make_async_remote_copy(
                    src_ref=send.at[step, side],
                    dst_ref=recv.at[step, side],
                    send_sem=face_send_sem.at[step, axis, side],
                    recv_sem=face_recv_sem.at[step, axis, side],
                    device_id=tuple(target),
                    device_id_type=MESH,
                )
                copies.append((copy, sends, gets))
        return copies

    def when_start(copy, sends):
        @pl.when(sends)
        def _():
            copy.start()

    all_copies = []
    for step in reversed(range(steps)):
        copies = face_copies(step)
        all_copies.extend(copies)
        flow_loads[step].wait()
        sum_ref[...] = adjoint
        last_x = pl.ds(brick_x - 1, brick_z, stride=brick_x)
        first_x = pl.ds(0, brick_z, stride=brick_x)
        last_z, first_z = pl.ds(lines - brick_x, brick_x), pl.ds(0, brick_x)
        flow = flow_ref[step]
        flow_y = courant_ref[1] * adjoint
        rise_y = jnp.where((flow & 2) != 0, flow_y, 0.0)
        fall_y = flow_y - rise_y
        edge = jnp.where(y_pos == 0, rise_y, jnp.where(y_pos == brick_y - 1, fall_y, 0.0))
        edge_high, edge_low = parts(edge)
        edge_rows = dot(take, edge_high, NT) + dot(take, edge_low, NT)
        for axis, send, ends in ((0, x_send, (first_x, last_x)), (2, z_send, (first_z, last_z))):
            for side, rows in enumerate(ends):
                up = (flow_ref[step, rows, :] & (1 << axis)) != 0
                leaving = up if side == 0 else jnp.logical_not(up)
                send[step, side] = jnp.where(
                    leaving, courant_ref[axis, rows, :] * sum_ref[rows, :], 0.0
                )
        y_send[step, 0] = edge_rows[0:ROWS]
        y_send[step, 1] = edge_rows[ROWS:2 * ROWS]
        for copy, sends, _ in copies:
            when_start(copy, sends)

        flow_x, flow_z = courant_ref[0] * adjoint, courant_ref[2] * adjoint
        rise_x = jnp.where((flow & 1) != 0, flow_x, 0.0)
        rise_z = jnp.where((flow & 4) != 0, flow_z, 0.0)
        rise = [rise_x, rise_y, rise_z]
        fall = [flow_x - rise_x, fall_y, flow_z - rise_z]
        rest = 1.0 - (courant_ref[0] + courant_ref[1] + courant_ref[2])
        updated = rest * adjoint
        updated = updated + jnp.where(
            x_pos == brick_x - 1, 0.0, pltpu.roll(rise[0], lines - 1, 0)
        )
        updated = updated + jnp.where(x_pos == 0, 0.0, pltpu.roll(fall[0], 1, 0))
        updated = updated + jnp.where(
            y_pos == brick_y - 1, 0.0, pltpu.roll(rise[1], brick_y - 1, 1)
        )
        updated = updated + jnp.where(y_pos == 0, 0.0, pltpu.roll(fall[1], 1, 1))
        border = jnp.zeros((brick_x, brick_y), jnp.float32)
        updated = updated + jnp.concatenate([rise[2][brick_x:], border], axis=0)
        updated = updated + jnp.concatenate([border, fall[2][:lines - brick_x]], axis=0)
        sum_ref[...] = updated

        for copy, _, gets in copies:
            @pl.when(gets)
            def _():
                copy.wait_recv()

        for rows, recv, side in (
            (last_x, x_recv, 0), (first_x, x_recv, 1), (last_z, z_recv, 0), (first_z, z_recv, 1)
        ):
            sum_ref[rows, :] = sum_ref[rows, :] + recv[step, side]
        side_rows = jnp.concatenate([y_recv[step, 0], y_recv[step, 1]], axis=0)
        side_high, side_low = parts(side_rows)
        adjoint = sum_ref[...] + (dot(side_high, put, TN) + dot(side_low, put, TN))
        tracer_loads[step].wait()
        if step == steps - 1:
            gradient = adjoint * tracer_ref[step]
        else:
            gradient = grad_ref[...] + adjoint * tracer_ref[step]
        grad_ref[...] = gradient

    high, low = parts(gradient)
    smooth_y = (
        dot(y_high[...], high, NT) + dot(y_low[...], high, NT) + dot(y_high[...], low, NT)
    )
    bulk_send[...] = smooth_y[0:shares * pad_rows]
    carries = smooth_y[shares * pad_rows:]
    packed = [
        carries[row:row + 1, t * LANES:(t + 1) * LANES] for row in (0, ROWS) for t in range(tiles)
    ]
    carry_send[...] = jnp.concatenate(packed, axis=0)
    carry_copies = []
    for d in range(1, n_gy):
        for moved, back in ((b + d, b - d), (b - d, b + d)):
            copy = pltpu.make_async_remote_copy(
                src_ref=carry_send,
                dst_ref=carry_recv.at[b],
                send_sem=carry_send_sem.at[rem(moved + n_gy, n_gy)],
                recv_sem=carry_recv_sem.at[b],
                device_id=(a, rem(moved + n_gy, n_gy), c),
                device_id_type=MESH,
            )
            arrival = pltpu.make_async_remote_copy(
                src_ref=carry_send,
                dst_ref=carry_recv.at[rem(back + n_gy, n_gy)],
                send_sem=carry_send_sem.at[rem(back + n_gy, n_gy)],
                recv_sem=carry_recv_sem.at[rem(back + n_gy, n_gy)],
                device_id=(a, rem(moved + n_gy, n_gy), c),
                device_id_type=MESH,
            )
            sends = (moved >= 0) & (moved < n_gy)
            gets = (back >= 0) & (back < n_gy)
            when_start(copy, sends)
            carry_copies.append((copy, sends, arrival, gets))

    mine = a * n_gz + c

    def far_first(d):
        return jnp.where(2 * b < n_gy, shares - 1 - d, d)

    def bulk_copy(d):
        share = far_first(d)
        other = b * shares + share
        return other, pltpu.make_async_remote_copy(
            src_ref=bulk_send.at[pl.ds(pl.multiple_of(share * pad_rows, ROWS), pad_rows), :],
            dst_ref=bulk_recv.at[mine],
            send_sem=bulk_send_sem.at[share],
            recv_sem=bulk_recv_sem.at[mine],
            device_id=(
                div(other, n_gy * n_gz), rem(div(other, n_gz), n_gy), rem(other, n_gz)
            ),
            device_id_type=MESH,
        )

    def bulk_start(d):
        other, copy = bulk_copy(d)

        @pl.when(other != me)
        def _():
            copy.start()

    each(0, shares, bulk_start)
    lambda_ref[...] = adjoint
    lambda_copy = pltpu.make_async_copy(lambda_ref, lambda_any, lambda_sem)
    lambda_copy.start()

    own = div(me, shares) == b

    @pl.when(own)
    def _():
        rows = pl.ds(pl.multiple_of((me - b * shares) * pad_rows, ROWS), pad_rows)
        bulk_recv[mine] = bulk_send[rows, :]

    for _, _, arrival, gets in carry_copies:
        @pl.when(gets)
        def _():
            arrival.wait_recv()

    carry_row = iota((2 * tiles, LANES), 0)
    entering = jnp.zeros((2 * tiles, LANES), jnp.float32)
    for brick in range(n_gy):
        between = jnp.where(carry_row < tiles, b - brick - 1, brick - b - 1)
        weight = jnp.exp(jnp.maximum(between, 0).astype(jnp.float32) * (-brick_y / length))
        entering = entering + jnp.where(between >= 0, weight, 0.0) * carry_recv[brick]
    enter_send[...] = entering

    def enter_copy(d):
        share = far_first(d)
        other = b * shares + share
        return other, pltpu.make_async_remote_copy(
            src_ref=enter_send,
            dst_ref=enter_recv.at[mine],
            send_sem=enter_send_sem.at[share],
            recv_sem=enter_recv_sem.at[mine],
            device_id=(
                div(other, n_gy * n_gz), rem(div(other, n_gz), n_gy), rem(other, n_gz)
            ),
            device_id_type=MESH,
        )

    def enter_start(d):
        other, copy = enter_copy(d)

        @pl.when(other != me)
        def _():
            copy.start()

    each(0, shares, enter_start)

    @pl.when(own)
    def _():
        enter_recv[mine] = enter_send[...]

    for copy, sends, _ in all_copies:
        @pl.when(sends)
        def _():
            copy.wait_send()

    for copy, sends, _, _ in carry_copies:
        @pl.when(sends)
        def _():
            copy.wait_send()

    at_y = rem(me, shares) * y_rows + iota((pad_rows, LANES), 0)
    from_low = jnp.exp(at_y.astype(jnp.float32) * (-1.0 / length))
    from_high = jnp.exp(jnp.maximum(brick_y - 1 - at_y, 0).astype(jnp.float32) * (-1.0 / length))
    for i in range(n_gx):
        for k in range(n_gz):
            slot = i * n_gz + k

            @pl.when(jnp.logical_not(own & (mine == slot)))
            def _():
                for send, recv, send_sem, recv_sem in (
                    (bulk_send.at[pl.ds(0, pad_rows), :], bulk_recv, bulk_send_sem, bulk_recv_sem),
                    (enter_send, enter_recv, enter_send_sem, enter_recv_sem),
                ):
                    pltpu.make_async_remote_copy(
                        src_ref=send,
                        dst_ref=recv.at[slot],
                        send_sem=send_sem.at[slot],
                        recv_sem=recv_sem.at[slot],
                        device_id=(a, b, c),
                        device_id_type=MESH,
                    ).wait_recv()

        rows = []
        for k in range(n_gz):
            slot = i * n_gz + k
            for t in range(tiles):
                rows.append(
                    bulk_recv[slot, :, t * LANES:(t + 1) * LANES]
                    + from_low * enter_recv[slot, t:t + 1, :]
                    + from_high * enter_recv[slot, tiles + t:tiles + t + 1, :]
                )
        high, low = parts(jnp.concatenate(rows, axis=0))
        block_high = table_high[i * LANES:(i + 1) * LANES, :]
        block_low = table_low[i * LANES:(i + 1) * LANES, :]
        product = dot(high, block_high, NN) + dot(low, block_high, NN) + dot(high, block_low, NN)
        wide_ref[...] = product if i == 0 else wide_ref[...] + product

    def bulk_sent(d):
        other, copy = bulk_copy(d)
        _, enter = enter_copy(d)

        @pl.when(other != me)
        def _():
            copy.wait_send()
            enter.wait_send()

    each(0, shares, bulk_sent)
    each(1, groups, well_sent)
    lambda_copy.wait()


def depth_kernel(
    sizes, lambda_ref, wide_ref, lambda_out, smooth_ref, stage_ref=None
):
    brick_z, full_z, full_x, y_rows, pad_rows, tile_z = sizes
    wide_x = lane_width(full_x)
    lambda_out[...] = lambda_ref[...]

    fade = math.exp(-0.5 / brick_z)

    def plane(z):
        row, depth = z // tile_z * pad_rows, z % tile_z
        start, shift = depth * wide_x // LANES * LANES, depth * wide_x % LANES
        here = wide_ref[row:row + y_rows, start:start + max(wide_x, LANES)]
        return pltpu.roll(here, LANES - shift, 1) if shift else here

    ahead = [plane(0)]
    for z in range(1, full_z):
        ahead.append(plane(z) + fade * ahead[-1])
    behind = None
    for z in reversed(range(full_z)):
        total = ahead[z] if behind is None else ahead[z] + behind
        if full_x <= LANES:
            smooth_ref[pl.ds(z, y_rows, stride=full_z), :] = total[:, 0:full_x]
        else:
            for tile in range(wide_x // LANES):
                part = total[:, tile * LANES:(tile + 1) * LANES]
                stage_ref[tile, pl.ds(z, y_rows, stride=full_z), :] = part
        behind = fade * (plane(z) if behind is None else plane(z) + behind)

    if full_x > LANES:
        for tile in range(wide_x // LANES):
            end = min((tile + 1) * LANES, full_x)
            smooth_ref[:, tile * LANES:end] = stage_ref[tile][:, 0:end - tile * LANES]


def per_device(well_sources, well_owner, well_cell, flow_sign, courant, tracer):
    steps, brick_z, brick_x, brick_y = tracer.shape
    n_gx, n_gy, n_gz = lax.axis_size("gx"), lax.axis_size("gy"), lax.axis_size("gz")
    groups, shares = n_gx * n_gy, n_gx * n_gz
    wells = well_cell.shape[0]
    cap = round_up(-(-wells // groups), ROWS)
    lines = brick_z * brick_x
    y_rows = brick_y // shares
    pad_rows = round_up(y_rows, ROWS)
    full_x, full_z = n_gx * brick_x, n_gz * brick_z
    wide_x = lane_width(full_x)
    tile_z = LANES // brick_x
    tiles = lines // LANES
    f32 = jnp.float32
    sizes = (n_gx, n_gy, n_gz, brick_z, brick_x, brick_y, cap)
    dma = pltpu.SemaphoreType.DMA
    vmem = pl.BlockSpec(memory_space=pltpu.VMEM)
    away = pl.BlockSpec(memory_space=pl.ANY)
    field = (3, lines, brick_y)
    stage = []
    if full_x > LANES:
        stage = [pltpu.VMEM((wide_x // LANES, y_rows * full_z, LANES), f32)]
    run = pl.pallas_call(
        functools.partial(kernel, sizes),
        out_shape=(
            jax.ShapeDtypeStruct((lines, brick_y), f32),
            jax.ShapeDtypeStruct((n_gz * tiles * pad_rows, tile_z * wide_x), f32),
        ),
        in_specs=[away] * 6,
        out_specs=(away, vmem),
        scratch_shapes=[
            pltpu.VMEM((lines, brick_y), f32),
            dma,
            pltpu.VMEM((brick_z, wells), f32),
            pltpu.VMEM((1, wells), jnp.int32),
            pltpu.VMEM((1, wells), jnp.int32),
            dma((3,)),
            pltpu.VMEM((steps, lines, brick_y), jnp.int32),
            pltpu.VMEM(field, f32),
            pltpu.VMEM((steps, lines, brick_y), f32),
            dma((2, steps + 1)),
            pltpu.VMEM((LANES, wells), f32),
            pltpu.VMEM((groups * cap, LANES), f32),
            pltpu.VMEM((groups * cap, LANES), f32),
            dma((groups,)),
            dma((groups,)),
            pltpu.VMEM((lines, brick_y), f32),
            pltpu.VMEM((lines, brick_y), f32),
            pltpu.VMEM((steps, 2, brick_z, brick_y), f32),
            pltpu.VMEM((steps, 2, brick_z, brick_y), f32),
            pltpu.VMEM((steps, 2, ROWS, lines), f32),
            pltpu.VMEM((steps, 2, ROWS, lines), f32),
            pltpu.VMEM((steps, 2, brick_x, brick_y), f32),
            pltpu.VMEM((steps, 2, brick_x, brick_y), f32),
            dma((steps, 3, 2)),
            dma((steps, 3, 2)),
            pltpu.VMEM((2 * tiles, LANES), f32),
            pltpu.VMEM((n_gy, 2 * tiles, LANES), f32),
            dma((n_gy,)),
            dma((n_gy,)),
            pltpu.VMEM((2 * tiles, LANES), f32),
            pltpu.VMEM((shares, 2 * tiles, LANES), f32),
            dma((shares,)),
            dma((shares,)),
            pltpu.VMEM((shares * pad_rows, lines), f32),
            pltpu.VMEM((shares, pad_rows, lines), f32),
            dma((shares,)),
            dma((shares,)),
            pltpu.VMEM((n_gx * LANES, tile_z * wide_x), jnp.bfloat16),
            pltpu.VMEM((n_gx * LANES, tile_z * wide_x), jnp.bfloat16),
            pltpu.VMEM((shares * pad_rows + 2 * ROWS, brick_y), jnp.bfloat16),
            pltpu.VMEM((shares * pad_rows + 2 * ROWS, brick_y), jnp.bfloat16),
        ],
        compiler_params=pltpu.CompilerParams(
            collective_id=0, has_side_effects=True, vmem_limit_bytes=56 * 2**20
        ),
    )
    start, wide = run(
        well_sources.T,
        well_owner.reshape(1, wells),
        well_cell.reshape(1, wells),
        flow_sign.reshape(steps, lines, brick_y),
        courant.reshape(field),
        tracer.reshape(steps, lines, brick_y),
    )
    depth_sizes = (brick_z, full_z, full_x, y_rows, pad_rows, tile_z)
    start, smoothed = pl.pallas_call(
        functools.partial(depth_kernel, depth_sizes),
        out_shape=(
            jax.ShapeDtypeStruct((lines, brick_y), f32),
            jax.ShapeDtypeStruct((y_rows * full_z, full_x), f32),
        ),
        in_specs=[vmem, vmem],
        out_specs=(vmem, vmem),
        scratch_shapes=stage,
    )(start, wide)
    return (
        start.reshape(brick_z, brick_x, brick_y),
        smoothed.reshape(y_rows, full_z, full_x),
    )


def solution(mesh):
    return jax.shard_map(
        per_device,
        mesh=mesh,
        in_specs=(
            P(("gx", "gy"), "gz"),
            P(("gx", "gy"), None),
            P(("gx", "gy")),
            P(None, "gz", "gx", "gy"),
            P(None, "gz", "gx", "gy"),
            P(None, "gz", "gx", "gy"),
        ),
        out_specs=(P("gz", "gx", "gy"), P(("gx", "gy", "gz"), None, None)),
        check_vma=False,
    )
```

```python
import functools
import math

import jax
import jax.numpy as jnp
from jax import lax
from jax.experimental import pallas as pl
from jax.experimental.pallas import tpu as pltpu
from jax.sharding import PartitionSpec as P

MESH = pl.DeviceIdType.MESH
LANES = 128
ROWS = 8


def round_up(value, unit):
    return -(-value // unit) * unit


def iota(shape, dim):
    return lax.broadcasted_iota(jnp.int32, shape, dim)


def div(value, by):
    return value >> (by.bit_length() - 1) if by & (by - 1) == 0 else lax.div(value, by)


def rem(value, by):
    return value & (by - 1) if by & (by - 1) == 0 else lax.rem(value, by)


def each(start, stop, act):
    if stop - start <= 32:
        for i in range(start, stop):
            act(i)
    else:
        lax.fori_loop(start, stop, lambda i, carried: (act(i), carried)[1], 0)


def parts(value):
    high = value.astype(jnp.bfloat16)
    return high, (value - high.astype(jnp.float32)).astype(jnp.bfloat16)


def lane_width(extent):
    return extent if LANES % extent == 0 else round_up(extent, LANES)


def dot(left, right, dims):
    return lax.dot_general(left, right, (dims, ((), ())), preferred_element_type=jnp.float32)


NN = ((1,), (0,))
NT = ((1,), (1,))
TN = ((0,), (0,))


def flag(mask):
    return jnp.where(mask, 1.0, 0.0).astype(jnp.bfloat16)


def dot_three(left, right, dims):
    left_high, left_low = parts(left)
    right_high, right_low = parts(right)
    return (
        dot(left_high, right_high, dims)
        + dot(left_low, right_high, dims)
        + dot(left_high, right_low, dims)
    )


def kernel(
    sizes, source_any, owner_any, cell_any, flow_any, courant_any, tracer_any,
    lambda_any, wide_ref, lambda_ref, lambda_sem,
    source_ref, owner_ref, cell_ref, small_sem,
    flow_ref, courant_ref, tracer_ref, load_sem,
    payload_ref, well_send, well_recv, well_send_sem, well_recv_sem,
    sum_ref, grad_ref,
    x_send, x_recv, y_send, y_recv, z_send, z_recv, face_send_sem, face_recv_sem,
    carry_send, carry_recv, carry_send_sem, carry_recv_sem,
    enter_send, enter_recv, enter_send_sem, enter_recv_sem,
    bulk_send, bulk_recv, bulk_send_sem, bulk_recv_sem,
    table_high, table_low, y_high, y_low,
):
    n_gx, n_gy, n_gz, brick_z, brick_x, brick_y, cap = sizes
    steps = flow_any.shape[0]
    length = 2.0 * brick_y
    lines = brick_z * brick_x
    groups = n_gx * n_gy
    devices = groups * n_gz
    a, b, c = lax.axis_index("gx"), lax.axis_index("gy"), lax.axis_index("gz")
    group = a * n_gy + b
    me = group * n_gz + c
    wells = source_any.shape[1]
    full_z = n_gz * brick_z
    full_x = n_gx * brick_x
    wide_x = lane_width(full_x)
    shares = n_gx * n_gz
    y_rows = brick_y // shares
    pad_rows = round_up(y_rows, ROWS)
    tiles = lines // LANES
    tile_z = LANES // brick_x

    for ref in (x_recv, y_recv, z_recv, carry_recv):
        ref[...] = jnp.zeros_like(ref)

    barrier = pltpu.get_barrier_semaphore()

    def greet(d):
        other = rem(me + d, devices)
        pl.semaphore_signal(
            barrier, inc=1,
            device_id=(
                div(other, n_gy * n_gz), rem(div(other, n_gz), n_gy), rem(other, n_gz)
            ),
            device_id_type=MESH,
        )

    each(1, devices, greet)
    small_loads = [
        pltpu.make_async_copy(src, dst, small_sem.at[i])
        for i, (src, dst) in enumerate(
            ((owner_any, owner_ref), (cell_any, cell_ref), (source_any, source_ref))
        )
    ]
    for load in small_loads:
        load.start()
    courant_load = pltpu.make_async_copy(courant_any, courant_ref, load_sem.at[0, steps])
    courant_load.start()
    flow_loads, tracer_loads = (
        [
            pltpu.make_async_copy(src.at[step], dst.at[step], load_sem.at[kind, step])
            for step in range(steps)
        ]
        for kind, (src, dst) in enumerate(((flow_any, flow_ref), (tracer_any, tracer_ref)))
    )
    for step in reversed(range(steps)):
        flow_loads[step].start()
        tracer_loads[step].start()

    eye = iota((wells, wells), 0) == iota((wells, wells), 1)
    before = iota((wells, wells), 0) < iota((wells, wells), 1)
    for load in small_loads:
        load.wait()
    owner_row = owner_ref[...].astype(jnp.float32)
    owner_col = jnp.sum(jnp.where(eye, owner_row, 0.0), axis=1, keepdims=True)
    rank_row = jnp.sum(
        jnp.where(before & (owner_col == owner_row), 1.0, 0.0), axis=0, keepdims=True
    )
    slots = groups * cap
    second = rank_row >= cap
    key_row = owner_row * cap + rank_row + jnp.where(second, slots - cap, 0)
    chosen = flag(iota((2 * slots, wells), 0) == key_row.astype(jnp.int32))
    cell_row = cell_ref[...]
    payload_ref[...] = jnp.zeros_like(payload_ref)
    payload_ref[0:brick_z, :] = source_ref[...]
    payload_ref[brick_z:brick_z + 1, :] = div(cell_row, brick_y).astype(jnp.float32)
    payload_ref[brick_z + 1:brick_z + 2, :] = rem(cell_row, brick_y).astype(jnp.float32)
    payload_high, payload_low = parts(payload_ref[...])
    sorted_wells = dot(chosen, payload_high, NT) + dot(chosen, payload_low, NT)
    well_send[...] = sorted_wells[0:slots] + pltpu.roll(sorted_wells[slots:], LANES // 2, 1)

    pl.semaphore_wait(barrier, devices - 1)

    def group_rows(index):
        return pl.ds(pl.multiple_of(index * cap, ROWS), cap)

    def well_copy(d):
        other = rem(group + d, groups)
        return pltpu.make_async_remote_copy(
            src_ref=well_send.at[group_rows(other), :],
            dst_ref=well_recv.at[group_rows(group), :],
            send_sem=well_send_sem.at[d],
            recv_sem=well_recv_sem.at[d],
            device_id=(div(other, n_gy), rem(other, n_gy), c),
            device_id_type=MESH,
        )

    def well_start(d):
        well_copy(d).start()

    each(1, groups, well_start)
    well_recv[group_rows(group), :] = well_send[group_rows(group), :]

    block = max(wide_x, LANES)
    shape = (n_gx * LANES, block)
    at_x = div(iota(shape, 0), LANES) * brick_x + rem(iota(shape, 0), brick_x)
    to_x = rem(iota(shape, 1), wide_x) if wide_x < LANES else iota(shape, 1)
    far = jnp.abs(at_x - to_x).astype(jnp.float32)
    table = jnp.exp(far * (-0.5 / brick_x)) / math.sqrt(2 * brick_x) / math.sqrt(2 * brick_z)
    table = jnp.where(to_x < full_x, table, 0.0)
    depth_of = rem(div(iota(shape, 0), brick_x), tile_z)
    if wide_x < LANES:
        depth_of = depth_of - div(iota(shape, 1), wide_x)
    for start in range(0, tile_z * wide_x, block):
        high, low = parts(jnp.where(depth_of == start // wide_x, table, 0.0))
        table_high[:, start:start + block] = high
        table_low[:, start:start + block] = low

    def line_place(row):
        return div(row, pad_rows) * y_rows + rem(row, pad_rows)

    shape = (shares * pad_rows, brick_y)
    near = jnp.abs(line_place(iota(shape, 0)) - iota(shape, 1)).astype(jnp.float32)
    table_y = jnp.exp(near * (-1.0 / length)) / math.sqrt(length)
    take_row, take_lane = iota((2 * ROWS, brick_y), 0), iota((2 * ROWS, brick_y), 1)
    from_end = jnp.where(take_row < ROWS, brick_y - take_lane, take_lane + 1)
    pull = jnp.exp(from_end.astype(jnp.float32) * (-1.0 / length)) / math.sqrt(length)
    y_high[...], y_low[...] = parts(jnp.concatenate([table_y, pull], axis=0))

    spread = flag(div(iota((lines, LANES), 0), brick_x) == iota((lines, LANES), 1))
    x_pick = flag(iota((ROWS, LANES), 1) == brick_z)

    courant_load.wait()

    def well_wait(d):
        well_copy(d).wait_recv()

    def well_sent(d):
        well_copy(d).wait_send()

    each(1, groups, well_wait)
    landed = well_recv[...]
    landed = jnp.concatenate([landed, pltpu.roll(landed, LANES // 2, 1)], axis=0)
    landed_high, landed_low = parts(landed)
    x_row = dot(x_pick, landed_high, NT)[0:1, :].astype(jnp.int32)
    x_hit = rem(iota((lines, 2 * slots), 0), brick_x) == x_row
    y_hit = flag(
        iota((2 * slots, LANES), 1) == landed[:, brick_z + 1:brick_z + 2].astype(jnp.int32)
    )
    spread_high = jnp.where(x_hit, dot(spread, landed_high, NT), 0.0).astype(jnp.bfloat16)
    spread_low = jnp.where(x_hit, dot(spread, landed_low, NT), 0.0).astype(jnp.bfloat16)
    adjoint = dot(spread_high, y_hit, NN) + dot(spread_low, y_hit, NN)

    y_pos = iota((lines, brick_y), 1)
    x_pos = rem(iota((lines, brick_y), 0), brick_x)
    take = flag(
        ((take_row < ROWS) & (take_lane == 0)) | ((take_row >= ROWS) & (take_lane == brick_y - 1))
    )
    put = flag(
        ((take_row == 0) & (take_lane == brick_y - 1)) | ((take_row == ROWS) & (take_lane == 0))
    )

    def face_copies(step):
        copies = []
        for axis, (place, count, send, recv) in enumerate(
            ((a, n_gx, x_send, x_recv), (b, n_gy, y_send, y_recv), (c, n_gz, z_send, z_recv))
        ):
            for side in range(2):
                moved = place - 1 if side == 0 else place + 1
                target = [a, b, c]
                target[axis] = rem(moved + count, count)
                sends = place > 0 if side == 0 else place < count - 1
                gets = place < count - 1 if side == 0 else place > 0
                copy = pltpu.make_async_remote_copy(
                    src_ref=send.at[step, side],
                    dst_ref=recv.at[step, side],
                    send_sem=face_send_sem.at[step, axis, side],
                    recv_sem=face_recv_sem.at[step, axis, side],
                    device_id=tuple(target),
                    device_id_type=MESH,
                )
                copies.append((copy, sends, gets))
        return copies

    def when_start(copy, sends):
        @pl.when(sends)
        def _():
            copy.start()

    all_copies = []
    for step in reversed(range(steps)):
        copies = face_copies(step)
        all_copies.extend(copies)
        flow_loads[step].wait()
        sum_ref[...] = adjoint
        last_x = pl.ds(brick_x - 1, brick_z, stride=brick_x)
        first_x = pl.ds(0, brick_z, stride=brick_x)
        last_z, first_z = pl.ds(lines - brick_x, brick_x), pl.ds(0, brick_x)
        flow = flow_ref[step]
        flow_y = courant_ref[1] * adjoint
        rise_y = jnp.where((flow & 2) != 0, flow_y, 0.0)
        fall_y = flow_y - rise_y
        edge = jnp.where(y_pos == 0, rise_y, jnp.where(y_pos == brick_y - 1, fall_y, 0.0))
        edge_high, edge_low = parts(edge)
        edge_rows = dot(take, edge_high, NT) + dot(take, edge_low, NT)
        for axis, send, ends in ((0, x_send, (first_x, last_x)), (2, z_send, (first_z, last_z))):
            for side, rows in enumerate(ends):
                up = (flow_ref[step, rows, :] & (1 << axis)) != 0
                leaving = up if side == 0 else jnp.logical_not(up)
                send[step, side] = jnp.where(
                    leaving, courant_ref[axis, rows, :] * sum_ref[rows, :], 0.0
                )
        y_send[step, 0] = edge_rows[0:ROWS]
        y_send[step, 1] = edge_rows[ROWS:2 * ROWS]
        for copy, sends, _ in copies:
            when_start(copy, sends)

        flow_x, flow_z = courant_ref[0] * adjoint, courant_ref[2] * adjoint
        rise_x = jnp.where((flow & 1) != 0, flow_x, 0.0)
        rise_z = jnp.where((flow & 4) != 0, flow_z, 0.0)
        rise = [rise_x, rise_y, rise_z]
        fall = [flow_x - rise_x, fall_y, flow_z - rise_z]
        rest = 1.0 - (courant_ref[0] + courant_ref[1] + courant_ref[2])
        updated = rest * adjoint
        updated = updated + jnp.where(
            x_pos == brick_x - 1, 0.0, pltpu.roll(rise[0], lines - 1, 0)
        )
        updated = updated + jnp.where(x_pos == 0, 0.0, pltpu.roll(fall[0], 1, 0))
        updated = updated + jnp.where(
            y_pos == brick_y - 1, 0.0, pltpu.roll(rise[1], brick_y - 1, 1)
        )
        updated = updated + jnp.where(y_pos == 0, 0.0, pltpu.roll(fall[1], 1, 1))
        border = jnp.zeros((brick_x, brick_y), jnp.float32)
        updated = updated + jnp.concatenate([rise[2][brick_x:], border], axis=0)
        updated = updated + jnp.concatenate([border, fall[2][:lines - brick_x]], axis=0)
        sum_ref[...] = updated

        for copy, _, gets in copies:
            @pl.when(gets)
            def _():
                copy.wait_recv()

        for rows, recv, side in (
            (last_x, x_recv, 0), (first_x, x_recv, 1), (last_z, z_recv, 0), (first_z, z_recv, 1)
        ):
            sum_ref[rows, :] = sum_ref[rows, :] + recv[step, side]
        side_rows = jnp.concatenate([y_recv[step, 0], y_recv[step, 1]], axis=0)
        side_high, side_low = parts(side_rows)
        adjoint = sum_ref[...] + (dot(side_high, put, TN) + dot(side_low, put, TN))
        tracer_loads[step].wait()
        if step == steps - 1:
            gradient = adjoint * tracer_ref[step]
        else:
            gradient = grad_ref[...] + adjoint * tracer_ref[step]
        grad_ref[...] = gradient

    high, low = parts(gradient)
    smooth_y = (
        dot(y_high[...], high, NT) + dot(y_low[...], high, NT) + dot(y_high[...], low, NT)
    )
    bulk_send[...] = smooth_y[0:shares * pad_rows]
    carries = smooth_y[shares * pad_rows:]
    mine = a * n_gz + c

    def far_first(d):
        return jnp.where(2 * b < n_gy, shares - 1 - d, d)

    def bulk_copy(d):
        share = far_first(d)
        other = b * shares + share
        return other, pltpu.make_async_remote_copy(
            src_ref=bulk_send.at[pl.ds(pl.multiple_of(share * pad_rows, ROWS), pad_rows), :],
            dst_ref=bulk_recv.at[mine],
            send_sem=bulk_send_sem.at[share],
            recv_sem=bulk_recv_sem.at[mine],
            device_id=(
                div(other, n_gy * n_gz), rem(div(other, n_gz), n_gy), rem(other, n_gz)
            ),
            device_id_type=MESH,
        )

    def bulk_start(d):
        other, copy = bulk_copy(d)

        @pl.when(other != me)
        def _():
            copy.start()

    each(0, shares, bulk_start)

    packed = [
        carries[row:row + 1, t * LANES:(t + 1) * LANES] for row in (0, ROWS) for t in range(tiles)
    ]
    carry_send[...] = jnp.concatenate(packed, axis=0)
    carry_copies = []
    for d in range(1, n_gy):
        for moved, back in ((b + d, b - d), (b - d, b + d)):
            copy = pltpu.make_async_remote_copy(
                src_ref=carry_send,
                dst_ref=carry_recv.at[b],
                send_sem=carry_send_sem.at[rem(moved + n_gy, n_gy)],
                recv_sem=carry_recv_sem.at[b],
                device_id=(a, rem(moved + n_gy, n_gy), c),
                device_id_type=MESH,
            )
            arrival = pltpu.make_async_remote_copy(
                src_ref=carry_send,
                dst_ref=carry_recv.at[rem(back + n_gy, n_gy)],
                send_sem=carry_send_sem.at[rem(back + n_gy, n_gy)],
                recv_sem=carry_recv_sem.at[rem(back + n_gy, n_gy)],
                device_id=(a, rem(moved + n_gy, n_gy), c),
                device_id_type=MESH,
            )
            sends = (moved >= 0) & (moved < n_gy)
            gets = (back >= 0) & (back < n_gy)
            when_start(copy, sends)
            carry_copies.append((copy, sends, arrival, gets))

    lambda_ref[...] = adjoint
    lambda_copy = pltpu.make_async_copy(lambda_ref, lambda_any, lambda_sem)
    lambda_copy.start()

    own = div(me, shares) == b

    @pl.when(own)
    def _():
        rows = pl.ds(pl.multiple_of((me - b * shares) * pad_rows, ROWS), pad_rows)
        bulk_recv[mine] = bulk_send[rows, :]

    for _, _, arrival, gets in carry_copies:
        @pl.when(gets)
        def _():
            arrival.wait_recv()

    carry_row = iota((2 * tiles, LANES), 0)
    entering = jnp.zeros((2 * tiles, LANES), jnp.float32)
    for brick in range(n_gy):
        between = jnp.where(carry_row < tiles, b - brick - 1, brick - b - 1)
        weight = jnp.exp(jnp.maximum(between, 0).astype(jnp.float32) * (-brick_y / length))
        entering = entering + jnp.where(between >= 0, weight, 0.0) * carry_recv[brick]
    enter_send[...] = entering

    def enter_copy(d):
        share = far_first(d)
        other = b * shares + share
        return other, pltpu.make_async_remote_copy(
            src_ref=enter_send,
            dst_ref=enter_recv.at[mine],
            send_sem=enter_send_sem.at[share],
            recv_sem=enter_recv_sem.at[mine],
            device_id=(
                div(other, n_gy * n_gz), rem(div(other, n_gz), n_gy), rem(other, n_gz)
            ),
            device_id_type=MESH,
        )

    def enter_start(d):
        other, copy = enter_copy(d)

        @pl.when(other != me)
        def _():
            copy.start()

    each(0, shares, enter_start)

    @pl.when(own)
    def _():
        enter_recv[mine] = enter_send[...]

    for copy, sends, _ in all_copies:
        @pl.when(sends)
        def _():
            copy.wait_send()

    for copy, sends, _, _ in carry_copies:
        @pl.when(sends)
        def _():
            copy.wait_send()

    at_y = rem(me, shares) * y_rows + iota((pad_rows, LANES), 0)
    from_low = jnp.exp(at_y.astype(jnp.float32) * (-1.0 / length))
    from_high = jnp.exp(jnp.maximum(brick_y - 1 - at_y, 0).astype(jnp.float32) * (-1.0 / length))
    for i in range(n_gx):
        for k in range(n_gz):
            slot = i * n_gz + k

            @pl.when(jnp.logical_not(own & (mine == slot)))
            def _():
                for send, recv, send_sem, recv_sem in (
                    (bulk_send.at[pl.ds(0, pad_rows), :], bulk_recv, bulk_send_sem, bulk_recv_sem),
                    (enter_send, enter_recv, enter_send_sem, enter_recv_sem),
                ):
                    pltpu.make_async_remote_copy(
                        src_ref=send,
                        dst_ref=recv.at[slot],
                        send_sem=send_sem.at[slot],
                        recv_sem=recv_sem.at[slot],
                        device_id=(a, b, c),
                        device_id_type=MESH,
                    ).wait_recv()

        rows = []
        for k in range(n_gz):
            slot = i * n_gz + k
            for t in range(tiles):
                rows.append(
                    bulk_recv[slot, :, t * LANES:(t + 1) * LANES]
                    + from_low * enter_recv[slot, t:t + 1, :]
                    + from_high * enter_recv[slot, tiles + t:tiles + t + 1, :]
                )
        high, low = parts(jnp.concatenate(rows, axis=0))
        block_high = table_high[i * LANES:(i + 1) * LANES, :]
        block_low = table_low[i * LANES:(i + 1) * LANES, :]
        product = dot(high, block_high, NN) + dot(low, block_high, NN) + dot(high, block_low, NN)
        wide_ref[...] = product if i == 0 else wide_ref[...] + product

    def bulk_sent(d):
        other, copy = bulk_copy(d)
        _, enter = enter_copy(d)

        @pl.when(other != me)
        def _():
            copy.wait_send()
            enter.wait_send()

    each(0, shares, bulk_sent)
    each(1, groups, well_sent)
    lambda_copy.wait()


def depth_kernel(
    sizes, lambda_ref, wide_ref, lambda_out, smooth_ref, stage_ref=None
):
    brick_z, full_z, full_x, y_rows, pad_rows, tile_z = sizes
    wide_x = lane_width(full_x)
    lambda_out[...] = lambda_ref[...]

    fade = math.exp(-0.5 / brick_z)

    def plane(z):
        row, depth = z // tile_z * pad_rows, z % tile_z
        start, shift = depth * wide_x // LANES * LANES, depth * wide_x % LANES
        here = wide_ref[row:row + y_rows, start:start + max(wide_x, LANES)]
        return pltpu.roll(here, LANES - shift, 1) if shift else here

    ahead = [plane(0)]
    for z in range(1, full_z):
        ahead.append(plane(z) + fade * ahead[-1])
    behind = None
    for z in reversed(range(full_z)):
        total = ahead[z] if behind is None else ahead[z] + behind
        if full_x <= LANES:
            smooth_ref[pl.ds(z, y_rows, stride=full_z), :] = total[:, 0:full_x]
        else:
            for tile in range(wide_x // LANES):
                part = total[:, tile * LANES:(tile + 1) * LANES]
                stage_ref[tile, pl.ds(z, y_rows, stride=full_z), :] = part
        behind = fade * (plane(z) if behind is None else plane(z) + behind)

    if full_x > LANES:
        for tile in range(wide_x // LANES):
            end = min((tile + 1) * LANES, full_x)
            smooth_ref[:, tile * LANES:end] = stage_ref[tile][:, 0:end - tile * LANES]


def per_device(well_sources, well_owner, well_cell, flow_sign, courant, tracer):
    steps, brick_z, brick_x, brick_y = tracer.shape
    n_gx, n_gy, n_gz = lax.axis_size("gx"), lax.axis_size("gy"), lax.axis_size("gz")
    groups, shares = n_gx * n_gy, n_gx * n_gz
    wells = well_cell.shape[0]
    cap = round_up(-(-wells // groups), ROWS)
    lines = brick_z * brick_x
    y_rows = brick_y // shares
    pad_rows = round_up(y_rows, ROWS)
    full_x, full_z = n_gx * brick_x, n_gz * brick_z
    wide_x = lane_width(full_x)
    tile_z = LANES // brick_x
    tiles = lines // LANES
    f32 = jnp.float32
    sizes = (n_gx, n_gy, n_gz, brick_z, brick_x, brick_y, cap)
    dma = pltpu.SemaphoreType.DMA
    vmem = pl.BlockSpec(memory_space=pltpu.VMEM)
    away = pl.BlockSpec(memory_space=pl.ANY)
    field = (3, lines, brick_y)
    stage = []
    if full_x > LANES:
        stage = [pltpu.VMEM((wide_x // LANES, y_rows * full_z, LANES), f32)]
    run = pl.pallas_call(
        functools.partial(kernel, sizes),
        out_shape=(
            jax.ShapeDtypeStruct((lines, brick_y), f32),
            jax.ShapeDtypeStruct((n_gz * tiles * pad_rows, tile_z * wide_x), f32),
        ),
        in_specs=[away] * 6,
        out_specs=(away, vmem),
        scratch_shapes=[
            pltpu.VMEM((lines, brick_y), f32),
            dma,
            pltpu.VMEM((brick_z, wells), f32),
            pltpu.VMEM((1, wells), jnp.int32),
            pltpu.VMEM((1, wells), jnp.int32),
            dma((3,)),
            pltpu.VMEM((steps, lines, brick_y), jnp.int32),
            pltpu.VMEM(field, f32),
            pltpu.VMEM((steps, lines, brick_y), f32),
            dma((2, steps + 1)),
            pltpu.VMEM((LANES, wells), f32),
            pltpu.VMEM((groups * cap, LANES), f32),
            pltpu.VMEM((groups * cap, LANES), f32),
            dma((groups,)),
            dma((groups,)),
            pltpu.VMEM((lines, brick_y), f32),
            pltpu.VMEM((lines, brick_y), f32),
            pltpu.VMEM((steps, 2, brick_z, brick_y), f32),
            pltpu.VMEM((steps, 2, brick_z, brick_y), f32),
            pltpu.VMEM((steps, 2, ROWS, lines), f32),
            pltpu.VMEM((steps, 2, ROWS, lines), f32),
            pltpu.VMEM((steps, 2, brick_x, brick_y), f32),
            pltpu.VMEM((steps, 2, brick_x, brick_y), f32),
            dma((steps, 3, 2)),
            dma((steps, 3, 2)),
            pltpu.VMEM((2 * tiles, LANES), f32),
            pltpu.VMEM((n_gy, 2 * tiles, LANES), f32),
            dma((n_gy,)),
            dma((n_gy,)),
            pltpu.VMEM((2 * tiles, LANES), f32),
            pltpu.VMEM((shares, 2 * tiles, LANES), f32),
            dma((shares,)),
            dma((shares,)),
            pltpu.VMEM((shares * pad_rows, lines), f32),
            pltpu.VMEM((shares, pad_rows, lines), f32),
            dma((shares,)),
            dma((shares,)),
            pltpu.VMEM((n_gx * LANES, tile_z * wide_x), jnp.bfloat16),
            pltpu.VMEM((n_gx * LANES, tile_z * wide_x), jnp.bfloat16),
            pltpu.VMEM((shares * pad_rows + 2 * ROWS, brick_y), jnp.bfloat16),
            pltpu.VMEM((shares * pad_rows + 2 * ROWS, brick_y), jnp.bfloat16),
        ],
        compiler_params=pltpu.CompilerParams(
            collective_id=0, has_side_effects=True, vmem_limit_bytes=56 * 2**20
        ),
    )
    start, wide = run(
        well_sources.T,
        well_owner.reshape(1, wells),
        well_cell.reshape(1, wells),
        flow_sign.reshape(steps, lines, brick_y),
        courant.reshape(field),
        tracer.reshape(steps, lines, brick_y),
    )
    depth_sizes = (brick_z, full_z, full_x, y_rows, pad_rows, tile_z)
    start, smoothed = pl.pallas_call(
        functools.partial(depth_kernel, depth_sizes),
        out_shape=(
            jax.ShapeDtypeStruct((lines, brick_y), f32),
            jax.ShapeDtypeStruct((y_rows * full_z, full_x), f32),
        ),
        in_specs=[vmem, vmem],
        out_specs=(vmem, vmem),
        scratch_shapes=stage,
    )(start, wide)
    return (
        start.reshape(brick_z, brick_x, brick_y),
        smoothed.reshape(y_rows, full_z, full_x),
    )


def solution(mesh):
    return jax.shard_map(
        per_device,
        mesh=mesh,
        in_specs=(
            P(("gx", "gy"), "gz"),
            P(("gx", "gy"), None),
            P(("gx", "gy")),
            P(None, "gz", "gx", "gy"),
            P(None, "gz", "gx", "gy"),
            P(None, "gz", "gx", "gy"),
        ),
        out_specs=(P("gz", "gx", "gy"), P(("gx", "gy", "gz"), None, None)),
        check_vma=False,
    )
```
